32 devices in a mesh: member: 8 (over y, x, core), tile: 4 (over z).
Axes of the slice: x: 2, y: 2, z: 4, core: 2. Of those that a mesh axis runs over, the one named last changes fastest.
Arguments:
- state: bfloat16 [64, 4, 32, 128], P('member', None, 'tile'), may hold values from -6 to 6
- first_weight: bfloat16 [32, 4, 3, 3], replicated, may hold values from -1 to 1
- middle_weight: bfloat16 [1, 32, 32, 3, 3], replicated, may hold values from -0.375 to 0.375
- last_weight: bfloat16 [4, 32, 3, 3], replicated, may hold values from -0.375 to 0.375
- observations: float32 [4, 8, 512], P('tile', 'member'), may hold values from -6 to 6
- obs_variance: float32 [4, 8, 512], P('tile', 'member'), may hold values from 0.5 to 4
- observation_rows: int32 [4, 8, 512], P('tile', 'member'), may hold values from 0 to 1535
- loc_class: int32 [4, 8, 512], P('tile', 'member'), may hold values from 0 to 7
Outputs:
- analysis: bfloat16 [64, 4, 32, 128], P('member', None, 'tile')
The draws below stay inside these ranges and needn't reach their ends.
Inputs may be any that keep to these rules, and one draw needn't show every extreme that they name: `observation_rows`: each observation of patch (t, j) reads one field at one point of the patches (t - 1, j), (t, j) or (t + 1, j), tiles taken cyclically.
All inputs are finite; a program needn't handle non-finite values.
Results may differ from the reference program's by a relative error of at most 0.0054.
Values may be sent and summed in bfloat16 or wider, within the bound.
A program may use at most 128 MiB of HBM per device.

```python
import math
import jax
import jax.numpy as jnp
from jax import lax

MEMBER_COUNT = 64
FIELD_COUNT = 4
C = 32
LAYERS = 3
NS_ITERS = 4
OBS = 512
W = 128
BAND_ROWS = 1
BANDS = 8
TILES = 4
NROWS = 32
PATCH = 128
N_MEMBER = 8
N_TILE = 4


def plant(entries, key, low, high):
    longest = entries.shape.index(max(entries.shape))
    spots = []
    for shift in (0, 1):
        where = [jax.random.randint(jax.random.fold_in(key, axis), (), 0, length) for axis, length in enumerate(entries.shape)]
        where[longest] = (where[longest] + shift) % entries.shape[longest]
        spots.append(tuple(where))
    return entries.at[spots[0]].set(low).at[spots[1]].set(high)


def block_levels(key, extent, pieces, low, largest):
    def one(axis_at, blocks):
        heights = jax.random.uniform(jax.random.fold_in(jax.random.fold_in(key, 6), axis_at), (blocks,), jnp.float32, low / len(pieces), largest / len(pieces))
        return jnp.repeat(jnp.exp(heights), extent[axis_at] // blocks).reshape((-1,) + (1,) * (len(extent) - axis_at - 1))

    gain = one(*pieces[0])
    for cut in pieces[1:]:
        gain = gain * one(*cut)
    return gain


def scatter_about(stream_key, dims, deviation, bound, cuts=(), held_as=jnp.bfloat16):
    gain = block_levels(stream_key, dims, cuts, -0.22, 0.18) if cuts else 1.0
    drawn = jax.random.normal(stream_key, dims, jnp.float32) * deviation * gain
    return jnp.minimum(jnp.maximum(drawn, -bound), bound).astype(held_as)


def setup_inputs(seed: int = 0) -> dict:
    splits = jax.random.split(jax.random.key(seed), 9)
    state = scatter_about(splits[0], (MEMBER_COUNT, FIELD_COUNT, NROWS, W), 1.0, 6.0, ((0, 8), (2, 4)))
    first_weight = scatter_about(splits[1], (C, FIELD_COUNT, 3, 3), (9 * FIELD_COUNT) ** -0.5, 1.0)
    middle_weight = scatter_about(splits[2], (LAYERS - 2, C, C, 3, 3), (9 * C) ** -0.5, 0.375)
    last_weight = scatter_about(splits[3], (FIELD_COUNT, C, 3, 3), (9 * C) ** -0.5, 0.375)
    observations = scatter_about(splits[4], (TILES, BANDS, OBS), 1.0, 6.0, ((0, 4), (1, 8)), jnp.float32)
    obs_variance = jnp.clip(jnp.exp(math.log(4.0) - 2.0794415 * jax.random.uniform(splits[5], (TILES, BANDS, OBS), jnp.float32) ** block_levels(splits[5], (TILES, BANDS, OBS), ((0, 4), (1, 8)), -0.2, 0.2)), 0.5, 4.0)
    observation_rows = plant(jax.random.randint(splits[6], (TILES, BANDS, OBS), 0, 3 * FIELD_COUNT * PATCH), jax.random.fold_in(splits[6], 1), 0, (3 * FIELD_COUNT * PATCH) - 1).astype(jnp.int32)
    loc_class = plant(jax.random.randint(splits[7], (TILES, BANDS, OBS), 0, 8), jax.random.fold_in(splits[7], 1), 0, 7).astype(jnp.int32)
    return {"state": state, "first_weight": first_weight, "middle_weight": middle_weight, "last_weight": last_weight, "observations": observations, "obs_variance": obs_variance, "observation_rows": observation_rows, "loc_class": loc_class}


def convolve(fields_in, weights):
    padded = jnp.pad(fields_in, ((0, 0), (0, 0), (1, 1), (1, 1)), mode='wrap')
    return lax.conv_general_dilated(padded, weights, (1, 1), 'VALID', dimension_numbers=('NCHW', 'OIHW', 'NCHW'), preferred_element_type=jnp.float32)

def step_forward(ensemble_state, first_weight, middle_weight, last_weight):
    single = ensemble_state[None]
    hidden = jax.nn.silu(convolve(single, first_weight)).astype(jnp.bfloat16)
    for middle in range(LAYERS - 2):
        hidden = jax.nn.silu(convolve(hidden, middle_weight[middle])).astype(jnp.bfloat16)
    element_count = convolve(hidden, last_weight)
    return (single.astype(jnp.float32) + element_count).astype(jnp.bfloat16)[0]

def analyse(neighbours, observed, variance, rows_read, classes):
    ensemble_size = neighbours.shape[1]
    span = neighbours.shape[2]
    source_part = rows_read // span
    offset = rows_read % span
    obs_ens = neighbours[source_part, :, offset].astype(jnp.float32)
    obs_mean = lax.optimization_barrier(jnp.mean(obs_ens, axis=1))
    obs_anom = obs_ens - obs_mean[:, None]
    obs_weight = jnp.exp(-0.25 * classes.astype(jnp.float32)) / variance
    identity = jnp.eye(ensemble_size, dtype=jnp.float32)
    highest = lax.Precision.HIGHEST
    gram = (ensemble_size - 1.0) * identity + jnp.dot(obs_anom.T, obs_weight[:, None] * obs_anom, precision=highest, preferred_element_type=jnp.float32)
    norm_scale = jnp.sqrt(jnp.sum(gram * gram))
    iterate_y = gram / norm_scale
    iterate_z = identity
    for sweep in range(NS_ITERS):
        middle_factor = 1.5 * identity - 0.5 * jnp.dot(iterate_z, iterate_y, precision=highest, preferred_element_type=jnp.float32)
        iterate_y = jnp.dot(iterate_y, middle_factor, precision=highest, preferred_element_type=jnp.float32)
        iterate_z = jnp.dot(middle_factor, iterate_z, precision=highest, preferred_element_type=jnp.float32)
    root_inv = iterate_z / jnp.sqrt(norm_scale)
    measurement_residual = jnp.dot(obs_anom.T, obs_weight * (observed - obs_mean), precision=highest, preferred_element_type=jnp.float32)
    mean_weights = jnp.dot(root_inv, jnp.dot(root_inv, measurement_residual, precision=highest, preferred_element_type=jnp.float32), precision=highest, preferred_element_type=jnp.float32)
    transform = jnp.sqrt(ensemble_size - 1.0) * root_inv + mean_weights[:, None]
    back = neighbours[1].astype(jnp.float32)
    back_mean = lax.optimization_barrier(jnp.mean(back, axis=0))
    back_anom = back - back_mean[None, :]
    result = back_mean[None, :] + jnp.dot(transform.T, back_anom, precision=highest, preferred_element_type=jnp.float32)
    return result.astype(jnp.bfloat16)

def reference(state, first_weight, middle_weight, last_weight, observations, obs_variance, observation_rows, loc_class):
    step_member_states = lax.map(lambda ensemble_state: step_forward(ensemble_state, first_weight, middle_weight, last_weight), state)
    grid_tiles = N_TILE
    row_bands = N_MEMBER
    points_per_patch = BAND_ROWS * W
    patch_grouped = step_member_states.reshape(MEMBER_COUNT, FIELD_COUNT, grid_tiles, row_bands, points_per_patch)
    patch_major = jnp.transpose(patch_grouped, (2, 3, 0, 1, 4))
    patch_ids = jnp.arange(grid_tiles * row_bands, dtype=jnp.int32)

    def one_patch(inputs):
        subdomain_index, observed, variance, rows_read, classes = inputs
        tile_now = subdomain_index // row_bands
        band_now = subdomain_index % row_bands
        tile_prev = (tile_now + grid_tiles - 1) % grid_tiles
        tile_next = (tile_now + 1) % grid_tiles
        neighbours = jnp.stack([patch_major[tile_prev, band_now], patch_major[tile_now, band_now], patch_major[tile_next, band_now]])
        neighbours = neighbours.reshape(3, MEMBER_COUNT, FIELD_COUNT * points_per_patch)
        return analyse(neighbours, observed, variance, rows_read, classes)
    analysed = lax.map(one_patch, (patch_ids, observations.reshape(grid_tiles * row_bands, OBS), obs_variance.reshape(grid_tiles * row_bands, OBS), observation_rows.reshape(grid_tiles * row_bands, OBS), loc_class.reshape(grid_tiles * row_bands, OBS)))
    analysed = analysed.reshape(grid_tiles, row_bands, MEMBER_COUNT, FIELD_COUNT, points_per_patch)
    analysed = jnp.transpose(analysed, (2, 3, 0, 1, 4))
    return analysed.reshape(MEMBER_COUNT, FIELD_COUNT, NROWS, W)
```

```python
import functools

import jax
import jax.numpy as jnp
import numpy as np
from jax import lax
from jax.experimental import pallas as pl
from jax.experimental.pallas import tpu as pltpu
from jax.sharding import PartitionSpec as P

NS_ITERS = 4
MESH = pl.DeviceIdType.MESH
F32 = jnp.float32
BF16 = jnp.bfloat16
HIGHEST = lax.Precision.HIGHEST


def silu(v):
    half = 0.5 * v
    return half + half * jnp.tanh(half)


def halo_selector(fields, rows, kept):
    pick = np.zeros((2, fields, kept, fields, rows), np.float32)
    for f in range(fields):
        for q in range(kept):
            pick[0, f, q, f, rows - kept + q] = 1
            pick[1, f, q, f, q] = 1
    return pick.reshape(2 * fields * kept, fields * rows)


def first_selector(fields, rows, kept, halo, out_rows, lanes):
    where = [(f, halo - kept + q) for f in range(fields) for q in range(kept)]
    where += [(f, halo + r) for f in range(fields) for r in range(rows)]
    where += [(f, halo + rows + q) for f in range(fields) for q in range(kept)]
    count = len(where)
    spread = np.zeros((3, fields, 3, out_rows, lanes), np.float32)
    for dx in range(3):
        for k, (f, row) in enumerate(where):
            for r in range(out_rows):
                if 0 <= row - r <= 2:
                    spread[dx, f, row - r, r, dx * count + k] = 1
    return spread.reshape(9 * fields, out_rows * lanes)


def dot(a, b, precision=None):
    return jnp.dot(a, b, precision=precision, preferred_element_type=F32)


def shifted(v):
    width = v.shape[1]
    return jnp.concatenate([pltpu.roll(v, 1, 1), v, pltpu.roll(v, width - 1, 1)], axis=0)


def kernel(
    sizes,
    state_ref, pick_ref, spread_ref, first_ref, last_ref, observed_ref, variance_ref, rows_ref, class_ref, *rest,
):
    n_member, n_tile, members, fields, rows, width, channels, depth, kept, lanes = sizes
    middle = depth - 2
    middle_refs = rest[:middle]
    out_ref = rest[middle]
    taps_first = rest[middle + 1]
    taps_middle = rest[middle + 2 : middle + 2 + middle]
    (
        taps_last, onehot, halo_out, halo_in, outbox, inbox, back_out, back_in,
        halo_send, halo_recv, fore_send, fore_recv, back_send, back_recv,
    ) = rest[middle + 2 + middle :]
    me = lax.axis_index("member")
    tile = lax.axis_index("tile")
    block = fields * rows
    ensemble = n_member * members
    span = fields * width

    def tile_at(shift):
        return lax.rem(tile + shift + n_tile, n_tile)

    def member_at(shift):
        return lax.rem(me + shift, n_member)

    barrier = pltpu.get_barrier_semaphore()
    peers = [(i, d) for d in (1, -1, 0) for i in range(n_member) if (i, d) != (0, 0)]
    for i, d in peers:
        pl.semaphore_signal(barrier, inc=1, device_id=(member_at(i), tile_at(d)), device_id_type=MESH)

    for m in range(members):
        edges = dot(pick_ref[...], state_ref[m]).astype(BF16)
        half = fields * kept
        halo_out[0, m] = edges[:half]
        halo_out[1, m] = edges[half:]
    pl.semaphore_wait(barrier, len(peers))
    halo_copies = []
    for side, d in ((0, 1), (1, -1)):
        copy = pltpu.make_async_remote_copy(
            src_ref=halo_out.at[side],
            dst_ref=halo_in.at[side],
            send_sem=halo_send.at[side],
            recv_sem=halo_recv.at[side],
            device_id=(me, tile_at(d)),
            device_id_type=MESH,
        )
        copy.start()
        halo_copies.append(copy)

    with jax.named_scope("taps"):
        wide = dot(first_ref[...], spread_ref[...]).astype(BF16)
        first_rows = rows + 2 * (depth - 1)
        count = taps_first.shape[1]
        for r in range(first_rows):
            taps_first[r * channels : (r + 1) * channels, :] = wide[:, r * lanes : r * lanes + count]
        for number in range(middle):
            in_rows = rows + 2 * (depth - 1 - number)
            inner = in_rows * channels
            padded = -(-inner // 128) * 128
            base = middle_refs[number][...].astype(F32)
            base = jnp.concatenate([base, jnp.zeros((base.shape[0], padded - base.shape[1]), F32)], axis=1)
            for r in range(in_rows - 2):
                moved = (pltpu.roll(base, r * channels, 1) if r else base).astype(BF16)
                for dx in range(3):
                    taps_middle[number][r * channels : (r + 1) * channels, dx * inner : (dx + 1) * inner] = moved[
                        dx * channels : (dx + 1) * channels, :inner
                    ]
        inner = (rows + 2) * channels
        padded = -(-inner // 128) * 128
        base = last_ref[...].astype(F32)
        base = jnp.concatenate([base, jnp.zeros((base.shape[0], padded - base.shape[1]), F32)], axis=1)
        row_of = lax.rem(lax.broadcasted_iota(jnp.int32, base.shape, 0), rows)
        total = jnp.where(row_of == 0, base, 0.0)
        for r in range(1, rows):
            total = total + jnp.where(row_of == r, pltpu.roll(base, r * channels, 1), 0.0)
        taps_last[...] = total.astype(BF16)[:, :inner]

    for copy in halo_copies:
        copy.wait_recv()

    group = 2 if members % 2 == 0 else 1
    forecasts = []
    for start in range(0, members, group):
        ids = range(start, start + group)
        own = [state_ref[m].astype(F32) for m in ids]
        stacked = [
            shifted(jnp.concatenate([halo_in[0, m].astype(F32), own[g], halo_in[1, m].astype(F32)], axis=0))
            for g, m in enumerate(ids)
        ]
        hidden = silu(dot(taps_first[...], jnp.concatenate(stacked, axis=1).astype(BF16)))
        for number in range(middle):
            stacked = [shifted(hidden[:, g * width : (g + 1) * width]).astype(BF16) for g in range(group)]
            hidden = silu(dot(taps_middle[number][...], jnp.concatenate(stacked, axis=1)))
        parts = dot(taps_last[...], hidden.astype(BF16))
        for g in range(group):
            part = parts[:, g * width : (g + 1) * width]
            change = part[block : 2 * block] + pltpu.roll(part[:block], 1, 1)
            change = change + pltpu.roll(part[2 * block :], width - 1, 1)
            forecasts.append(own[g] + change)

    per_field = []
    for f in range(fields):
        cube = jnp.stack([v[f * rows : (f + 1) * rows] for v in forecasts], axis=0)
        per_field.append(jnp.transpose(cube, (1, 0, 2)))
    for r in range(rows):
        outbox[r] = jnp.concatenate([cube[r] for cube in per_field], axis=0).astype(BF16)

    fore_copies = {}
    for s in (0, 2, 1):
        for i in range(n_member):
            if s == 1 and i == 0:
                continue
            target = member_at(i)
            copy = pltpu.make_async_remote_copy(
                src_ref=outbox.at[target],
                dst_ref=inbox.at[s, me],
                send_sem=fore_send.at[s, i],
                recv_sem=fore_recv.at[s, i],
                device_id=(target, tile_at(1 - s)),
                device_id_type=MESH,
            )
            copy.start()
            fore_copies[s, i] = copy
    inbox[1, me] = outbox[me]

    read = rows_ref[...]
    spot = lax.broadcasted_iota(jnp.int32, (span, read.shape[1]), 0)
    for s in range(3):
        onehot[s] = jnp.where(spot == read - s * span, 1.0, 0.0).astype(BF16)
    obs_weight = jnp.exp(-0.25 * class_ref[...].astype(F32)) / variance_ref[...]
    eye_row = lax.broadcasted_iota(jnp.int32, (ensemble, ensemble), 0)
    eye_col = lax.broadcasted_iota(jnp.int32, (ensemble, ensemble), 1)
    identity = jnp.where(eye_row == eye_col, 1.0, 0.0).astype(F32)

    def neighbour(s):
        blocks = [inbox[s, k].astype(F32) for k in range(n_member)]
        columns = [
            jnp.concatenate([b[f * members : (f + 1) * members] for b in blocks], axis=0) for f in range(fields)
        ]
        return jnp.concatenate(columns, axis=1)

    obs_ens = None
    back = None
    for s in (1, 0, 2):
        for i in range(n_member):
            if (s, i) in fore_copies:
                fore_copies[s, i].wait_recv()
        values = neighbour(s)
        if s == 1:
            back = values
        part = dot(values.astype(BF16), onehot[s])
        obs_ens = part if obs_ens is None else obs_ens + part

    obs_mean = jnp.sum(obs_ens, axis=0, keepdims=True) / ensemble
    obs_anom = obs_ens - obs_mean
    gram = (ensemble - 1.0) * identity + lax.dot_general(
        obs_anom, obs_weight * obs_anom, (((1,), (1,)), ((), ())), precision=HIGHEST, preferred_element_type=F32
    )
    residual = jnp.sum(obs_anom * (obs_weight * (observed_ref[...] - obs_mean)), axis=1, keepdims=True)
    norm_scale = jnp.sqrt(jnp.sum(gram * gram, keepdims=True))
    iterate_y = gram / norm_scale
    iterate_z = 1.5 * identity - 0.5 * iterate_y
    iterate_y = dot(iterate_y, iterate_z, HIGHEST)
    for sweep in range(1, NS_ITERS):
        factor = 1.5 * identity - 0.5 * dot(iterate_z, iterate_y, HIGHEST)
        if sweep + 1 < NS_ITERS:
            iterate_y = dot(iterate_y, factor, HIGHEST)
        iterate_z = dot(factor, iterate_z, HIGHEST)
    root_inv = iterate_z / jnp.sqrt(norm_scale)
    back_mean = jnp.sum(back, axis=0, keepdims=True) / ensemble
    back_anom = back - back_mean
    moved = dot(root_inv, back_anom, HIGHEST)
    pull = dot(root_inv, jnp.broadcast_to(residual, (ensemble, 128)), HIGHEST)[:, :1]
    shift = back_mean + jnp.sum(pull * moved, axis=0, keepdims=True)
    analysed = shift + (ensemble - 1.0) ** 0.5 * moved

    for k in range(n_member):
        rows_k = analysed[k * members : (k + 1) * members]
        back_out[k] = jnp.concatenate(
            [rows_k[:, f * width : (f + 1) * width] for f in range(fields)], axis=0
        ).astype(BF16)
    back_copies = []
    for i in range(1, n_member):
        target = member_at(i)
        copy = pltpu.make_async_remote_copy(
            src_ref=back_out.at[target],
            dst_ref=back_in.at[me],
            send_sem=back_send.at[i],
            recv_sem=back_recv.at[i],
            device_id=(target, tile),
            device_id_type=MESH,
        )
        copy.start()
        back_copies.append(copy)
    back_in[me] = back_out[me]
    for copy in halo_copies:
        copy.wait_send()
    for copy in fore_copies.values():
        copy.wait_send()
    for copy in back_copies:
        copy.wait_recv()
    landed = [back_in[r].astype(F32) for r in range(rows)]
    per_field = []
    for f in range(fields):
        cube = jnp.stack([v[f * members : (f + 1) * members] for v in landed], axis=0)
        per_field.append(jnp.transpose(cube, (1, 0, 2)))
    for m in range(members):
        out_ref[m] = jnp.concatenate([cube[m] for cube in per_field], axis=0).astype(BF16)
    for copy in back_copies:
        copy.wait_send()


def local(state, first_weight, middle_weight, last_weight, observations, obs_variance, observation_rows, loc_class):
    members, fields, rows, width = state.shape
    channels = first_weight.shape[0]
    middle = middle_weight.shape[0]
    depth = middle + 2
    n_member = lax.axis_size("member")
    n_tile = lax.axis_size("tile")
    assert rows == n_member and n_tile >= 3
    kept = depth
    while fields * kept % 16:
        kept += 1
    assert kept <= rows
    block = fields * rows
    first_rows = rows + 2 * (depth - 1)
    count = 3 * (block + 2 * fields * kept)
    lanes = -(-count // 128) * 128
    obs = observations.shape[2]
    span = fields * width
    pick = jnp.asarray(halo_selector(fields, rows, kept), BF16)
    spread = jnp.asarray(first_selector(fields, rows, kept, depth, first_rows, lanes), BF16)
    first_taps = jnp.transpose(first_weight, (0, 3, 1, 2)).reshape(channels, 9 * fields)
    middle_taps = [
        jnp.transpose(middle_weight[n], (3, 0, 2, 1)).reshape(3 * channels, 3 * channels) for n in range(middle)
    ]
    last_taps = jnp.repeat(jnp.transpose(last_weight, (3, 0, 2, 1)).reshape(3 * fields, 3 * channels), rows, axis=0)
    sizes = (n_member, n_tile, members, fields, rows, width, channels, depth, kept, lanes)
    vmem = pl.BlockSpec(memory_space=pltpu.VMEM)
    packet = (fields * members, width)
    out = pl.pallas_call(
        functools.partial(kernel, sizes),
        out_shape=jax.ShapeDtypeStruct((members, block, width), BF16),
        in_specs=[vmem] * (9 + middle),
        out_specs=vmem,
        scratch_shapes=[
            pltpu.VMEM((first_rows * channels, count), BF16),
            *[
                pltpu.VMEM(
                    ((rows + 2 * (depth - 2 - n)) * channels, 3 * (rows + 2 * (depth - 1 - n)) * channels), BF16
                )
                for n in range(middle)
            ],
            pltpu.VMEM((3 * block, (rows + 2) * channels), BF16),
            pltpu.VMEM((3, span, obs), BF16),
            pltpu.VMEM((2, members, fields * kept, width), BF16),
            pltpu.VMEM((2, members, fields * kept, width), BF16),
            pltpu.VMEM((n_member, *packet), BF16),
            pltpu.VMEM((3, n_member, *packet), BF16),
            pltpu.VMEM((n_member, *packet), BF16),
            pltpu.VMEM((n_member, *packet), BF16),
            pltpu.SemaphoreType.DMA((2,)),
            pltpu.SemaphoreType.DMA((2,)),
            pltpu.SemaphoreType.DMA((3, n_member)),
            pltpu.SemaphoreType.DMA((3, n_member)),
            pltpu.SemaphoreType.DMA((n_member,)),
            pltpu.SemaphoreType.DMA((n_member,)),
        ],
        compiler_params=pltpu.CompilerParams(
            collective_id=0, has_side_effects=True, vmem_limit_bytes=40 * 1024 * 1024
        ),
    )(
        state.reshape(members, block, width), pick, spread, first_taps, last_taps,
        observations[0], obs_variance[0], observation_rows[0], loc_class[0], *middle_taps,
    )
    return out.reshape(members, fields, rows, width)


def solution(mesh):
    return jax.shard_map(
        local,
        mesh=mesh,
        in_specs=(
            P("member", None, "tile", None),
            P(),
            P(),
            P(),
            P("tile", "member", None),
            P("tile", "member", None),
            P("tile", "member", None),
            P("tile", "member", None),
        ),
        out_specs=P("member", None, "tile", None),
        check_vma=False,
    )
```

```python
import functools

import jax
import jax.numpy as jnp
import numpy as np
from jax import lax
from jax.experimental import pallas as pl
from jax.experimental.pallas import tpu as pltpu
from jax.sharding import PartitionSpec as P

NS_ITERS = 4
MESH = pl.DeviceIdType.MESH
F32 = jnp.float32
BF16 = jnp.bfloat16


def silu(v):
    half = 0.5 * v
    return half + half * jnp.tanh(half)


def first_selector(fields, rows, kept, halo, out_rows, lanes):
    where = [(f, halo - kept + q) for f in range(fields) for q in range(kept)]
    where += [(f, halo + r) for f in range(fields) for r in range(rows)]
    where += [(f, halo + rows + q) for f in range(fields) for q in range(kept)]
    count = len(where)
    spread = np.zeros((3, 3, fields, out_rows, lanes), np.float32)
    for dx in range(3):
        for k, (f, row) in enumerate(where):
            for r in range(out_rows):
                if 0 <= row - r <= 2:
                    spread[row - r, dx, f, r, dx * count + k] = 1
    return spread.reshape(9 * fields, out_rows * lanes)


def dot(a, b):
    return jnp.dot(a, b, preferred_element_type=F32)


def split(v):
    high = v.astype(BF16)
    return high, (v - high.astype(F32)).astype(BF16)


def dot_split(a, b):
    a_high, a_low = split(a)
    b_high, b_low = split(b)
    return dot(jnp.concatenate([a_high, a_low, a_high], axis=1), jnp.concatenate([b_high, b_high, b_low], axis=0))


def shifted(v):
    width = v.shape[1]
    return jnp.concatenate([pltpu.roll(v, 1, 1), v, pltpu.roll(v, width - 1, 1)], axis=0)


def tap_rows(load, padded):
    lines = []
    for dx in range(3):
        parts = [load(3 * dy + dx) for dy in range(3)]
        filler = jnp.zeros((parts[0].shape[0], padded - 3 * parts[0].shape[1]), F32)
        lines.append(jnp.concatenate([*parts, filler], axis=1))
    return jnp.concatenate(lines, axis=0)


def kernel(sizes, *refs):
    n_member, n_tile, members, fields, rows, width, channels, depth, kept, lanes = sizes
    middle = depth - 2
    sources, out_ref, refs = refs[:9], refs[9], refs[10:]
    fetched, refs = refs[:9], refs[9:]
    (
        state_ref, spread_ref, first_ref, middle_ref, last_ref, observed_ref, variance_ref, rows_ref, class_ref,
    ) = fetched
    taps_first, taps_middle, refs = refs[0], refs[1 : 1 + middle], refs[1 + middle :]
    (
        taps_last, onehot, halo_out, halo_in, outbox, inbox, back_out, back_in, fetch_sem,
        halo_send, halo_recv, fore_send, fore_recv, back_send, back_recv,
    ) = refs
    fetches = [
        pltpu.make_async_copy(source, target, fetch_sem.at[n])
        for n, (source, target) in enumerate(zip(sources, fetched))
    ]
    fetches[0].start()
    me = lax.axis_index("member")
    tile = lax.axis_index("tile")
    block = fields * rows
    ensemble = n_member * members
    span = fields * width

    def tile_at(shift):
        return lax.rem(tile + shift + n_tile, n_tile)

    def member_at(shift):
        return lax.rem(me + shift, n_member)

    barrier = pltpu.get_barrier_semaphore()
    peers = [(i, d) for d in (1, -1, 0) for i in range(n_member) if (i, d) != (0, 0)]
    for i, d in peers:
        pl.semaphore_signal(barrier, inc=1, device_id=(member_at(i), tile_at(d)), device_id_type=MESH)

    for fetch in fetches[1:]:
        fetch.start()
    fetches[0].wait()
    for m in range(members):
        whole = state_ref[m].astype(F32)
        each = [whole[f * rows : (f + 1) * rows] for f in range(fields)]
        halo_out[0, m] = jnp.concatenate([v[rows - kept :] for v in each], axis=0).astype(BF16)
        halo_out[1, m] = jnp.concatenate([v[:kept] for v in each], axis=0).astype(BF16)
    pl.semaphore_wait(barrier, len(peers))
    halo_copies = []
    for side, d in ((0, 1), (1, -1)):
        copy = pltpu.make_async_remote_copy(
            src_ref=halo_out.at[side],
            dst_ref=halo_in.at[side],
            send_sem=halo_send.at[side],
            recv_sem=halo_recv.at[side],
            device_id=(me, tile_at(d)),
            device_id_type=MESH,
        )
        copy.start()
        halo_copies.append(copy)

    with jax.named_scope("taps"):
        for fetch in fetches[1:]:
            fetch.wait()
        first_taps = jnp.concatenate([first_ref[n].astype(F32) for n in range(9)], axis=0).astype(BF16)
        wide = lax.dot_general(
            first_taps, spread_ref[...], (((0,), (0,)), ((), ())), preferred_element_type=F32
        ).astype(BF16)
        first_rows = rows + 2 * (depth - 1)
        count = taps_first.shape[1]
        for r in range(first_rows):
            taps_first[r * channels : (r + 1) * channels, :] = wide[:, r * lanes : r * lanes + count]
        for number in range(middle):
            in_rows = rows + 2 * (depth - 1 - number)
            inner = in_rows * channels
            padded = -(-inner // 128) * 128
            base = tap_rows(lambda n: middle_ref[9 * number + n].astype(F32), padded)
            for r in range(in_rows - 2):
                moved = (pltpu.roll(base, r * channels, 1) if r else base).astype(BF16)
                for dx in range(3):
                    taps_middle[number][r * channels : (r + 1) * channels, dx * inner : (dx + 1) * inner] = moved[
                        dx * channels : (dx + 1) * channels, :inner
                    ]
        inner = (rows + 2) * channels
        padded = -(-inner // 128) * 128
        base = tap_rows(lambda n: last_ref[n].astype(F32), padded)
        base = jnp.broadcast_to(base[:, None, :], (base.shape[0], rows, padded)).reshape(-1, padded)
        row_of = lax.rem(lax.broadcasted_iota(jnp.int32, base.shape, 0), rows)
        total = jnp.where(row_of == 0, base, 0.0)
        for r in range(1, rows):
            total = total + jnp.where(row_of == r, pltpu.roll(base, r * channels, 1), 0.0)
        taps_last[...] = total.astype(BF16)[:, :inner]

    for copy in halo_copies:
        copy.wait_recv()

    group = 2 if members % 2 == 0 else 1
    forecasts = []
    for start in range(0, members, group):
        ids = range(start, start + group)
        own = [state_ref[m].astype(F32) for m in ids]
        stacked = [
            shifted(jnp.concatenate([halo_in[0, m].astype(F32), own[g], halo_in[1, m].astype(F32)], axis=0))
            for g, m in enumerate(ids)
        ]
        hidden = silu(dot(taps_first[...], jnp.concatenate(stacked, axis=1).astype(BF16)))
        for number in range(middle):
            stacked = [shifted(hidden[:, g * width : (g + 1) * width]).astype(BF16) for g in range(group)]
            hidden = silu(dot(taps_middle[number][...], jnp.concatenate(stacked, axis=1)))
        parts = dot(taps_last[...], hidden.astype(BF16))
        for g in range(group):
            part = parts[:, g * width : (g + 1) * width]
            change = part[block : 2 * block] + pltpu.roll(part[:block], 1, 1)
            change = change + pltpu.roll(part[2 * block :], width - 1, 1)
            forecasts.append(own[g] + change)

    per_field = []
    for f in range(fields):
        cube = jnp.stack([v[f * rows : (f + 1) * rows] for v in forecasts], axis=0)
        per_field.append(jnp.transpose(cube, (1, 0, 2)))
    for r in range(rows):
        outbox[r] = jnp.concatenate([cube[r] for cube in per_field], axis=0).astype(BF16)

    fore_copies = {}
    for s in (0, 2, 1):
        for i in range(n_member):
            if s == 1 and i == 0:
                continue
            target = member_at(i)
            copy = pltpu.make_async_remote_copy(
                src_ref=outbox.at[target],
                dst_ref=inbox.at[s, me],
                send_sem=fore_send.at[s, i],
                recv_sem=fore_recv.at[s, i],
                device_id=(target, tile_at(1 - s)),
                device_id_type=MESH,
            )
            copy.start()
            fore_copies[s, i] = copy
    inbox[1, me] = outbox[me]

    read = rows_ref[...]
    spot = lax.broadcasted_iota(jnp.int32, (span, read.shape[1]), 0)
    for s in range(3):
        onehot[s] = jnp.where(spot == read - s * span, 1.0, 0.0).astype(BF16)
    obs_weight = jnp.exp(-0.25 * class_ref[...].astype(F32)) / variance_ref[...]
    eye_row = lax.broadcasted_iota(jnp.int32, (ensemble, ensemble), 0)
    eye_col = lax.broadcasted_iota(jnp.int32, (ensemble, ensemble), 1)
    identity = jnp.where(eye_row == eye_col, 1.0, 0.0).astype(F32)

    def neighbour(s):
        blocks = [inbox[s, k].astype(F32) for k in range(n_member)]
        columns = [
            jnp.concatenate([b[f * members : (f + 1) * members] for b in blocks], axis=0) for f in range(fields)
        ]
        return jnp.concatenate(columns, axis=1)

    obs_ens = None
    back = None
    for s in (1, 0, 2):
        for i in range(n_member):
            if (s, i) in fore_copies:
                fore_copies[s, i].wait_recv()
        values = neighbour(s)
        if s == 1:
            back = values
        part = dot(values.astype(BF16), onehot[s])
        obs_ens = part if obs_ens is None else obs_ens + part

    obs_mean = jnp.sum(obs_ens, axis=0, keepdims=True) / ensemble
    obs_anom = obs_ens - obs_mean
    anom_high, anom_low = split(obs_anom)
    heavy_high, heavy_low = split(obs_weight * obs_anom)
    gram = (ensemble - 1.0) * identity + lax.dot_general(
        jnp.concatenate([anom_high, anom_low, anom_high], axis=1),
        jnp.concatenate([heavy_high, heavy_high, heavy_low], axis=1),
        (((1,), (1,)), ((), ())),
        preferred_element_type=F32,
    )
    residual = jnp.sum(obs_anom * (obs_weight * (observed_ref[...] - obs_mean)), axis=1, keepdims=True)
    norm_scale = jnp.sqrt(jnp.sum(gram * gram, keepdims=True))
    iterate_y = gram / norm_scale
    iterate_z = 1.5 * identity - 0.5 * iterate_y
    iterate_y = dot_split(iterate_y, iterate_z)
    for sweep in range(1, NS_ITERS):
        factor = 1.5 * identity - 0.5 * dot_split(iterate_z, iterate_y)
        if sweep + 1 < NS_ITERS:
            iterate_y = dot_split(iterate_y, factor)
        iterate_z = dot_split(factor, iterate_z)
    root_inv = iterate_z / jnp.sqrt(norm_scale)
    back_mean = jnp.sum(back, axis=0, keepdims=True) / ensemble
    back_anom = back - back_mean
    both = dot_split(root_inv, jnp.concatenate([back_anom, jnp.broadcast_to(residual, (ensemble, 128))], axis=1))
    moved, pull = both[:, :span], both[:, span : span + 1]
    shift = back_mean + jnp.sum(pull * moved, axis=0, keepdims=True)
    analysed = shift + (ensemble - 1.0) ** 0.5 * moved

    for k in range(n_member):
        rows_k = analysed[k * members : (k + 1) * members]
        back_out[k] = jnp.concatenate(
            [rows_k[:, f * width : (f + 1) * width] for f in range(fields)], axis=0
        ).astype(BF16)
    back_copies = []
    for i in range(1, n_member):
        target = member_at(i)
        copy = pltpu.make_async_remote_copy(
            src_ref=back_out.at[target],
            dst_ref=back_in.at[me],
            send_sem=back_send.at[i],
            recv_sem=back_recv.at[i],
            device_id=(target, tile),
            device_id_type=MESH,
        )
        copy.start()
        back_copies.append(copy)
    back_in[me] = back_out[me]
    for copy in halo_copies:
        copy.wait_send()
    for copy in fore_copies.values():
        copy.wait_send()
    for copy in back_copies:
        copy.wait_recv()
    landed = [back_in[r].astype(F32) for r in range(rows)]
    per_field = []
    for f in range(fields):
        cube = jnp.stack([v[f * members : (f + 1) * members] for v in landed], axis=0)
        per_field.append(jnp.transpose(cube, (1, 0, 2)))
    for m in range(members):
        out_ref[m] = jnp.concatenate([cube[m] for cube in per_field], axis=0).astype(BF16)
    for copy in back_copies:
        copy.wait_send()


def local(state, first_weight, middle_weight, last_weight, observations, obs_variance, observation_rows, loc_class):
    members, fields, rows, width = state.shape
    channels = first_weight.shape[0]
    middle = middle_weight.shape[0]
    depth = middle + 2
    n_member = lax.axis_size("member")
    n_tile = lax.axis_size("tile")
    assert rows == n_member and n_tile >= 3
    kept = depth
    while fields * kept % 16:
        kept += 1
    assert kept <= rows
    block = fields * rows
    first_rows = rows + 2 * (depth - 1)
    count = 3 * (block + 2 * fields * kept)
    lanes = -(-count // 128) * 128
    obs = observations.shape[2]
    span = fields * width
    spread = jnp.asarray(first_selector(fields, rows, kept, depth, first_rows, lanes), BF16)
    operands = (
        state.reshape(members, block, width),
        spread,
        jnp.transpose(first_weight, (2, 3, 1, 0)).reshape(9, fields, channels),
        jnp.transpose(middle_weight, (0, 3, 4, 1, 2)).reshape(9 * middle, channels, channels),
        jnp.transpose(last_weight, (2, 3, 0, 1)).reshape(9, fields, channels),
        observations[0],
        obs_variance[0],
        observation_rows[0],
        loc_class[0],
    )
    sizes = (n_member, n_tile, members, fields, rows, width, channels, depth, kept, lanes)
    vmem = pl.BlockSpec(memory_space=pltpu.VMEM)
    packet = (fields * members, width)
    out = pl.pallas_call(
        functools.partial(kernel, sizes),
        out_shape=jax.ShapeDtypeStruct((members, block, width), BF16),
        in_specs=[pl.BlockSpec(memory_space=pltpu.HBM)] * len(operands),
        out_specs=vmem,
        scratch_shapes=[
            *[pltpu.VMEM(v.shape, v.dtype) for v in operands],
            pltpu.VMEM((first_rows * channels, count), BF16),
            *[
                pltpu.VMEM(
                    ((rows + 2 * (depth - 2 - n)) * channels, 3 * (rows + 2 * (depth - 1 - n)) * channels), BF16
                )
                for n in range(middle)
            ],
            pltpu.VMEM((3 * block, (rows + 2) * channels), BF16),
            pltpu.VMEM((3, span, obs), BF16),
            pltpu.VMEM((2, members, fields * kept, width), BF16),
            pltpu.VMEM((2, members, fields * kept, width), BF16),
            pltpu.VMEM((n_member, *packet), BF16),
            pltpu.VMEM((3, n_member, *packet), BF16),
            pltpu.VMEM((n_member, *packet), BF16),
            pltpu.VMEM((n_member, *packet), BF16),
            pltpu.SemaphoreType.DMA((len(operands),)),
            pltpu.SemaphoreType.DMA((2,)),
            pltpu.SemaphoreType.DMA((2,)),
            pltpu.SemaphoreType.DMA((3, n_member)),
            pltpu.SemaphoreType.DMA((3, n_member)),
            pltpu.SemaphoreType.DMA((n_member,)),
            pltpu.SemaphoreType.DMA((n_member,)),
        ],
        compiler_params=pltpu.CompilerParams(
            collective_id=0, has_side_effects=True, vmem_limit_bytes=60 * 1024 * 1024
        ),
    )(*operands)
    return out.reshape(members, fields, rows, width)


def solution(mesh):
    return jax.shard_map(
        local,
        mesh=mesh,
        in_specs=(
            P("member", None, "tile", None),
            P(),
            P(),
            P(),
            P("tile", "member", None),
            P("tile", "member", None),
            P("tile", "member", None),
            P("tile", "member", None),
        ),
        out_specs=P("member", None, "tile", None),
        check_vma=False,
    )
```

```python
import functools

import jax
import jax.numpy as jnp
import numpy as np
from jax import lax
from jax.experimental import pallas as pl
from jax.experimental.pallas import tpu as pltpu
from jax.sharding import PartitionSpec as P

NS_ITERS = 4
MESH = pl.DeviceIdType.MESH
F32 = jnp.float32
BF16 = jnp.bfloat16


def silu(v):
    half = 0.5 * v
    return half + half * jnp.tanh(half)


def first_selector(fields, rows, kept, halo, out_rows, lanes):
    where = [(f, halo - kept + q) for f in range(fields) for q in range(kept)]
    where += [(f, halo + r) for f in range(fields) for r in range(rows)]
    where += [(f, halo + rows + q) for f in range(fields) for q in range(kept)]
    count = len(where)
    spread = np.zeros((3, 3, fields, out_rows, lanes), np.float32)
    for dx in range(3):
        for k, (f, row) in enumerate(where):
            for r in range(out_rows):
                if 0 <= row - r <= 2:
                    spread[row - r, dx, f, r, dx * count + k] = 1
    return spread.reshape(9 * fields, out_rows * lanes)


def dot(a, b):
    return jnp.dot(a, b, preferred_element_type=F32)


def split(v):
    high = v.astype(BF16)
    return high, (v - high.astype(F32)).astype(BF16)


def dot_split(a, b):
    a_high, a_low = split(a)
    b_high, b_low = split(b)
    return dot(jnp.concatenate([a_high, a_low, a_high], axis=1), jnp.concatenate([b_high, b_high, b_low], axis=0))


def shifted(v):
    width = v.shape[1]
    return jnp.concatenate([pltpu.roll(v, 1, 1), v, pltpu.roll(v, width - 1, 1)], axis=0)


def tap_rows(load, padded):
    lines = []
    for dx in range(3):
        parts = [load(3 * dy + dx) for dy in range(3)]
        filler = jnp.zeros((parts[0].shape[0], padded - 3 * parts[0].shape[1]), F32)
        lines.append(jnp.concatenate([*parts, filler], axis=1))
    return jnp.concatenate(lines, axis=0)


def kernel(sizes, *refs):
    n_member, n_tile, members, fields, rows, width, channels, depth, kept, lanes, halves = sizes
    middle = depth - 2
    sources, out_ref, refs = refs[:9], refs[9], refs[10:]
    fetched, refs = refs[:9], refs[9:]
    (
        state_ref, spread_ref, first_ref, middle_ref, last_ref, observed_ref, variance_ref, rows_ref, class_ref,
    ) = fetched
    taps_first, taps_middle, refs = refs[0], refs[1 : 1 + middle], refs[1 + middle :]
    (
        taps_last, onehot, halo_out, halo_in, outbox, inbox, back_out, back_in, fetch_sem,
        halo_send, halo_recv, fore_send, fore_recv, back_send, back_recv,
    ) = refs
    fetches = [
        pltpu.make_async_copy(source, target, fetch_sem.at[n])
        for n, (source, target) in enumerate(zip(sources, fetched))
    ]
    fetches[0].start()
    me = lax.axis_index("member")
    tile = lax.axis_index("tile")
    block = fields * rows
    ensemble = n_member * members
    span = fields * width

    def tile_at(shift):
        return lax.rem(tile + shift + n_tile, n_tile)

    def member_at(shift):
        return lax.rem(me + shift, n_member)

    barrier = pltpu.get_barrier_semaphore()
    peers = [(i, d) for d in (1, -1, 0) for i in range(n_member) if (i, d) != (0, 0)]
    for i, d in peers:
        pl.semaphore_signal(barrier, inc=1, device_id=(member_at(i), tile_at(d)), device_id_type=MESH)

    for fetch in fetches[1:]:
        fetch.start()
    fetches[0].wait()
    for m in range(members):
        whole = state_ref[m].astype(F32)
        each = [whole[f * rows : (f + 1) * rows] for f in range(fields)]
        halo_out[0, m] = jnp.concatenate([v[rows - kept :] for v in each], axis=0).astype(BF16)
        halo_out[1, m] = jnp.concatenate([v[:kept] for v in each], axis=0).astype(BF16)
    pl.semaphore_wait(barrier, len(peers))
    halo_copies = []
    for side, d in ((0, 1), (1, -1)):
        copy = pltpu.make_async_remote_copy(
            src_ref=halo_out.at[side],
            dst_ref=halo_in.at[side],
            send_sem=halo_send.at[side],
            recv_sem=halo_recv.at[side],
            device_id=(me, tile_at(d)),
            device_id_type=MESH,
        )
        copy.start()
        halo_copies.append(copy)

    with jax.named_scope("taps"):
        for fetch in fetches[1:]:
            fetch.wait()
        first_taps = jnp.concatenate([first_ref[n].astype(F32) for n in range(9)], axis=0).astype(BF16)
        wide = lax.dot_general(
            first_taps, spread_ref[...], (((0,), (0,)), ((), ())), preferred_element_type=F32
        ).astype(BF16)
        first_rows = rows + 2 * (depth - 1)
        count = taps_first.shape[1]
        for r in range(first_rows):
            taps_first[r * channels : (r + 1) * channels, :] = wide[:, r * lanes : r * lanes + count]
        for number in range(middle):
            in_rows = rows + 2 * (depth - 1 - number)
            inner = in_rows * channels
            padded = -(-inner // 128) * 128
            base = tap_rows(lambda n: middle_ref[9 * number + n].astype(F32), padded)
            for r in range(in_rows - 2):
                moved = (pltpu.roll(base, r * channels, 1) if r else base).astype(BF16)
                for dx in range(3):
                    taps_middle[number][r * channels : (r + 1) * channels, dx * inner : (dx + 1) * inner] = moved[
                        dx * channels : (dx + 1) * channels, :inner
                    ]
        inner = (rows + 2) * channels
        padded = -(-inner // 128) * 128
        base = tap_rows(lambda n: last_ref[n].astype(F32), padded)
        base = jnp.broadcast_to(base[:, None, :], (base.shape[0], rows, padded)).reshape(-1, padded)
        row_of = lax.rem(lax.broadcasted_iota(jnp.int32, base.shape, 0), rows)
        total = jnp.where(row_of == 0, base, 0.0)
        for r in range(1, rows):
            total = total + jnp.where(row_of == r, pltpu.roll(base, r * channels, 1), 0.0)
        taps_last[...] = total.astype(BF16)[:, :inner]

    for copy in halo_copies:
        copy.wait_recv()

    share = members // halves
    group = 2 if share % 2 == 0 else 1
    fore_copies = {}
    for half in range(halves):
        forecasts = []
        for start in range(half * share, (half + 1) * share, group):
            ids = range(start, start + group)
            own = [state_ref[m].astype(F32) for m in ids]
            stacked = [
                shifted(jnp.concatenate([halo_in[0, m].astype(F32), own[g], halo_in[1, m].astype(F32)], axis=0))
                for g, m in enumerate(ids)
            ]
            hidden = silu(dot(taps_first[...], jnp.concatenate(stacked, axis=1).astype(BF16)))
            for number in range(middle):
                stacked = [shifted(hidden[:, g * width : (g + 1) * width]).astype(BF16) for g in range(group)]
                hidden = silu(dot(taps_middle[number][...], jnp.concatenate(stacked, axis=1)))
            parts = dot(taps_last[...], hidden.astype(BF16))
            for g in range(group):
                part = parts[:, g * width : (g + 1) * width]
                change = part[block : 2 * block] + pltpu.roll(part[:block], 1, 1)
                change = change + pltpu.roll(part[2 * block :], width - 1, 1)
                forecasts.append(own[g] + change)

        per_field = []
        for f in range(fields):
            cube = jnp.stack([v[f * rows : (f + 1) * rows] for v in forecasts], axis=0)
            per_field.append(jnp.transpose(cube, (1, 0, 2)))
        for r in range(rows):
            outbox[half, r] = jnp.concatenate([cube[r] for cube in per_field], axis=0).astype(BF16)

        for s in (0, 2, 1):
            for i in range(n_member):
                if s == 1 and i == 0:
                    continue
                target = member_at(i)
                copy = pltpu.make_async_remote_copy(
                    src_ref=outbox.at[half, target],
                    dst_ref=inbox.at[s, half, me],
                    send_sem=fore_send.at[s, half, i],
                    recv_sem=fore_recv.at[s, half, i],
                    device_id=(target, tile_at(1 - s)),
                    device_id_type=MESH,
                )
                copy.start()
                fore_copies[s, half, i] = copy
        inbox[1, half, me] = outbox[half, me]

    read = rows_ref[...]
    spot = lax.broadcasted_iota(jnp.int32, (span, read.shape[1]), 0)
    for s in range(3):
        onehot[s] = jnp.where(spot == read - s * span, 1.0, 0.0).astype(BF16)
    obs_weight = jnp.exp(-0.25 * class_ref[...].astype(F32)) / variance_ref[...]
    eye_row = lax.broadcasted_iota(jnp.int32, (ensemble, ensemble), 0)
    eye_col = lax.broadcasted_iota(jnp.int32, (ensemble, ensemble), 1)
    identity = jnp.where(eye_row == eye_col, 1.0, 0.0).astype(F32)

    def neighbour(s):
        blocks = [inbox[s, half, k].astype(F32) for k in range(n_member) for half in range(halves)]
        columns = [
            jnp.concatenate([b[f * share : (f + 1) * share] for b in blocks], axis=0) for f in range(fields)
        ]
        return jnp.concatenate(columns, axis=1)

    obs_ens = None
    back = None
    for s in (1, 0, 2):
        for half in range(halves):
            for i in range(n_member):
                if (s, half, i) in fore_copies:
                    fore_copies[s, half, i].wait_recv()
        values = neighbour(s)
        if s == 1:
            back = values
        part = dot(values.astype(BF16), onehot[s])
        obs_ens = part if obs_ens is None else obs_ens + part

    obs_mean = jnp.sum(obs_ens, axis=0, keepdims=True) / ensemble
    obs_anom = obs_ens - obs_mean
    anom_high, anom_low = split(obs_anom)
    heavy_high, heavy_low = split(obs_weight * obs_anom)
    gram = (ensemble - 1.0) * identity + lax.dot_general(
        jnp.concatenate([anom_high, anom_low, anom_high], axis=1),
        jnp.concatenate([heavy_high, heavy_high, heavy_low], axis=1),
        (((1,), (1,)), ((), ())),
        preferred_element_type=F32,
    )
    residual = jnp.sum(obs_anom * (obs_weight * (observed_ref[...] - obs_mean)), axis=1, keepdims=True)
    norm_scale = jnp.sqrt(jnp.sum(gram * gram, keepdims=True))
    iterate_y = gram / norm_scale
    iterate_z = 1.5 * identity - 0.5 * iterate_y
    iterate_y = dot_split(iterate_y, iterate_z)
    for sweep in range(1, NS_ITERS):
        factor = 1.5 * identity - 0.5 * dot_split(iterate_z, iterate_y)
        if sweep + 1 < NS_ITERS:
            iterate_y = dot_split(iterate_y, factor)
        iterate_z = dot_split(factor, iterate_z)
    root_inv = iterate_z / jnp.sqrt(norm_scale)
    back_mean = jnp.sum(back, axis=0, keepdims=True) / ensemble
    back_anom = back - back_mean
    both = dot_split(root_inv, jnp.concatenate([back_anom, jnp.broadcast_to(residual, (ensemble, 128))], axis=1))
    moved, pull = both[:, :span], both[:, span : span + 1]
    shift = back_mean + jnp.sum(pull * moved, axis=0, keepdims=True)
    analysed = shift + (ensemble - 1.0) ** 0.5 * moved

    for k in range(n_member):
        rows_k = analysed[k * members : (k + 1) * members]
        back_out[k] = jnp.concatenate(
            [rows_k[:, f * width : (f + 1) * width] for f in range(fields)], axis=0
        ).astype(BF16)
    back_copies = []
    for i in range(1, n_member):
        target = member_at(i)
        copy = pltpu.make_async_remote_copy(
            src_ref=back_out.at[target],
            dst_ref=back_in.at[me],
            send_sem=back_send.at[i],
            recv_sem=back_recv.at[i],
            device_id=(target, tile),
            device_id_type=MESH,
        )
        copy.start()
        back_copies.append(copy)
    back_in[me] = back_out[me]
    for copy in halo_copies:
        copy.wait_send()
    for copy in fore_copies.values():
        copy.wait_send()
    for copy in back_copies:
        copy.wait_recv()
    landed = [back_in[r].astype(F32) for r in range(rows)]
    per_field = []
    for f in range(fields):
        cube = jnp.stack([v[f * members : (f + 1) * members] for v in landed], axis=0)
        per_field.append(jnp.transpose(cube, (1, 0, 2)))
    for m in range(members):
        out_ref[m] = jnp.concatenate([cube[m] for cube in per_field], axis=0).astype(BF16)
    for copy in back_copies:
        copy.wait_send()


def local(state, first_weight, middle_weight, last_weight, observations, obs_variance, observation_rows, loc_class):
    members, fields, rows, width = state.shape
    channels = first_weight.shape[0]
    middle = middle_weight.shape[0]
    depth = middle + 2
    n_member = lax.axis_size("member")
    n_tile = lax.axis_size("tile")
    assert rows == n_member and n_tile >= 3
    kept = depth
    while fields * kept % 16:
        kept += 1
    assert kept <= rows
    block = fields * rows
    first_rows = rows + 2 * (depth - 1)
    count = 3 * (block + 2 * fields * kept)
    lanes = -(-count // 128) * 128
    obs = observations.shape[2]
    span = fields * width
    spread = jnp.asarray(first_selector(fields, rows, kept, depth, first_rows, lanes), BF16)
    operands = (
        state.reshape(members, block, width),
        spread,
        jnp.transpose(first_weight, (2, 3, 1, 0)).reshape(9, fields, channels),
        jnp.transpose(middle_weight, (0, 3, 4, 1, 2)).reshape(9 * middle, channels, channels),
        jnp.transpose(last_weight, (2, 3, 0, 1)).reshape(9, fields, channels),
        observations[0],
        obs_variance[0],
        observation_rows[0],
        loc_class[0],
    )
    halves = 2 if members % 2 == 0 and (fields * members // 2) % 16 == 0 else 1
    sizes = (n_member, n_tile, members, fields, rows, width, channels, depth, kept, lanes, halves)
    vmem = pl.BlockSpec(memory_space=pltpu.VMEM)
    packet = (fields * members, width)
    out = pl.pallas_call(
        functools.partial(kernel, sizes),
        out_shape=pltpu.VMEM((members, block, width), BF16),
        in_specs=[pl.BlockSpec(memory_space=pltpu.HBM)] * len(operands),
        out_specs=vmem,
        scratch_shapes=[
            *[pltpu.VMEM(v.shape, v.dtype) for v in operands],
            pltpu.VMEM((first_rows * channels, count), BF16),
            *[
                pltpu.VMEM(
                    ((rows + 2 * (depth - 2 - n)) * channels, 3 * (rows + 2 * (depth - 1 - n)) * channels), BF16
                )
                for n in range(middle)
            ],
            pltpu.VMEM((3 * block, (rows + 2) * channels), BF16),
            pltpu.VMEM((3, span, obs), BF16),
            pltpu.VMEM((2, members, fields * kept, width), BF16),
            pltpu.VMEM((2, members, fields * kept, width), BF16),
            pltpu.VMEM((halves, n_member, fields * members // halves, width), BF16),
            pltpu.VMEM((3, halves, n_member, fields * members // halves, width), BF16),
            pltpu.VMEM((n_member, *packet), BF16),
            pltpu.VMEM((n_member, *packet), BF16),
            pltpu.SemaphoreType.DMA((len(operands),)),
            pltpu.SemaphoreType.DMA((2,)),
            pltpu.SemaphoreType.DMA((2,)),
            pltpu.SemaphoreType.DMA((3, halves, n_member)),
            pltpu.SemaphoreType.DMA((3, halves, n_member)),
            pltpu.SemaphoreType.DMA((n_member,)),
            pltpu.SemaphoreType.DMA((n_member,)),
        ],
        compiler_params=pltpu.CompilerParams(
            collective_id=0, has_side_effects=True, vmem_limit_bytes=60 * 1024 * 1024
        ),
    )(*operands)
    return out.reshape(members, fields, rows, width)


def solution(mesh):
    return jax.shard_map(
        local,
        mesh=mesh,
        in_specs=(
            P("member", None, "tile", None),
            P(),
            P(),
            P(),
            P("tile", "member", None),
            P("tile", "member", None),
            P("tile", "member", None),
            P("tile", "member", None),
        ),
        out_specs=P("member", None, "tile", None),
        check_vma=False,
    )
```

```python
import functools

import jax
import jax.numpy as jnp
import numpy as np
from jax import lax
from jax.experimental import pallas as pl
from jax.experimental.pallas import tpu as pltpu
from jax.sharding import PartitionSpec as P

NS_ITERS = 4
MESH = pl.DeviceIdType.MESH
F32 = jnp.float32
BF16 = jnp.bfloat16


def silu(v):
    half = 0.5 * v
    return half + half * jnp.tanh(half)


def first_selector(fields, rows, kept, halo, out_rows, lanes):
    where = [(f, halo - kept + q) for f in range(fields) for q in range(kept)]
    where += [(f, halo + r) for f in range(fields) for r in range(rows)]
    where += [(f, halo + rows + q) for f in range(fields) for q in range(kept)]
    count = len(where)
    spread = np.zeros((3, 3, fields, out_rows, lanes), np.float32)
    for dx in range(3):
        for k, (f, row) in enumerate(where):
            for r in range(out_rows):
                if 0 <= row - r <= 2:
                    spread[row - r, dx, f, r, dx * count + k] = 1
    return spread.reshape(9 * fields, out_rows * lanes)


def dot(a, b):
    return jnp.dot(a, b, preferred_element_type=F32)


def split(v):
    high = v.astype(BF16)
    return high, (v - high.astype(F32)).astype(BF16)


def dot_split(a_twice, b):
    high, low = split(a_twice)
    size = a_twice.shape[0]
    lane = lax.broadcasted_iota(jnp.int32, a_twice.shape, 1)
    mixed = jnp.where(lane < size, high.astype(F32), low.astype(F32)).astype(BF16)
    b_high, b_low = split(b)
    return dot(jnp.concatenate([mixed, mixed], axis=1), jnp.concatenate([b_high, b_high, b_low, b_low], axis=0))


def shifted(v):
    width = v.shape[1]
    return jnp.concatenate([pltpu.roll(v, 1, 1), v, pltpu.roll(v, width - 1, 1)], axis=0)


def gathered(parts, width):
    third = parts.shape[0] // 3
    sums = []
    for at in range(0, parts.shape[1], width):
        part = parts[:, at : at + width]
        left, right = pltpu.roll(part[:third], 1, 1), pltpu.roll(part[2 * third :], width - 1, 1)
        sums.append(part[third : 2 * third] + left + right)
    return jnp.concatenate(sums, axis=1)


def tap_rows(load, padded):
    lines = []
    for dx in range(3):
        parts = [load(3 * dy + dx) for dy in range(3)]
        filler = jnp.zeros((parts[0].shape[0], padded - 3 * parts[0].shape[1]), F32)
        lines.append(jnp.concatenate([*parts, filler], axis=1))
    return jnp.concatenate(lines, axis=0)


def kernel(sizes, *refs):
    n_member, n_tile, members, fields, rows, width, channels, depth, kept, lanes, halves, chunks = sizes
    middle = depth - 2
    sources, out_ref, refs = refs[:9], refs[9], refs[10:]
    fetched, refs = refs[:9], refs[9:]
    (
        state_ref, spread_ref, first_ref, middle_ref, last_ref, observed_ref, variance_ref, rows_ref, class_ref,
    ) = fetched
    taps_first, taps_middle, refs = refs[0], refs[1 : 1 + middle], refs[1 + middle :]
    (
        taps_last, onehot, halo_out, halo_in, outbox, inbox, back_out, back_in, fetch_sem,
        halo_send, halo_recv, fore_send, fore_recv, back_send, back_recv,
    ) = refs
    fetches = [
        pltpu.make_async_copy(source, target, fetch_sem.at[n])
        for n, (source, target) in enumerate(zip(sources, fetched))
    ]
    fetches[0].start()
    me = lax.axis_index("member")
    tile = lax.axis_index("tile")
    block = fields * rows
    ensemble = n_member * members
    span = fields * width

    def wrapped(index, count):
        index = jnp.where(index >= count, index - count, index)
        return jnp.where(index < 0, index + count, index)

    def tile_at(shift):
        return wrapped(tile + shift, n_tile) if shift else tile

    def member_at(shift):
        return wrapped(me + shift, n_member) if shift else me

    barrier = pltpu.get_barrier_semaphore()
    peers = [(i, d) for d in (1, -1, 0) for i in range(n_member) if (i, d) != (0, 0)]
    for i, d in peers:
        pl.semaphore_signal(barrier, inc=1, device_id=(member_at(i), tile_at(d)), device_id_type=MESH)

    for fetch in fetches[1:]:
        fetch.start()
    fetches[0].wait()
    for m in range(members):
        whole = state_ref[m].astype(F32)
        each = [whole[f * rows : (f + 1) * rows] for f in range(fields)]
        halo_out[0, m] = jnp.concatenate([v[rows - kept :] for v in each], axis=0).astype(BF16)
        halo_out[1, m] = jnp.concatenate([v[:kept] for v in each], axis=0).astype(BF16)
    pl.semaphore_wait(barrier, len(peers))
    halo_copies = []
    for side, d in ((0, 1), (1, -1)):
        copy = pltpu.make_async_remote_copy(
            src_ref=halo_out.at[side],
            dst_ref=halo_in.at[side],
            send_sem=halo_send.at[side],
            recv_sem=halo_recv.at[side],
            device_id=(me, tile_at(d)),
            device_id_type=MESH,
        )
        copy.start()
        halo_copies.append(copy)

    with jax.named_scope("taps"):
        for fetch in fetches[1:]:
            fetch.wait()
        first_taps = jnp.concatenate([first_ref[n].astype(F32) for n in range(9)], axis=0).astype(BF16)
        wide = lax.dot_general(
            first_taps, spread_ref[...], (((0,), (0,)), ((), ())), preferred_element_type=F32
        ).astype(BF16)
        first_rows = rows + 2 * (depth - 1)
        count = taps_first.shape[1]
        for r in range(first_rows):
            taps_first[r * channels : (r + 1) * channels, :] = wide[:, r * lanes : r * lanes + count]
        for number in range(middle):
            chunk = chunks[number]
            inner = (chunk + 2) * channels
            padded = -(-inner // 128) * 128
            base = tap_rows(lambda n: middle_ref[9 * number + n].astype(F32), padded)
            for r in range(chunk):
                moved = (pltpu.roll(base, r * channels, 1) if r else base).astype(BF16)
                for dx in range(3):
                    at = (dx * chunk + r) * channels
                    taps_middle[number][at : at + channels, :] = moved[dx * channels : (dx + 1) * channels, :inner]
        inner = (rows + 2) * channels
        padded = -(-inner // 128) * 128
        base = tap_rows(lambda n: last_ref[n].astype(F32), padded)
        base = jnp.broadcast_to(base[:, None, :], (base.shape[0], rows, padded)).reshape(-1, padded)
        row_of = lax.rem(lax.broadcasted_iota(jnp.int32, base.shape, 0), rows)
        total = jnp.where(row_of == 0, base, 0.0)
        for r in range(1, rows):
            total = total + jnp.where(row_of == r, pltpu.roll(base, r * channels, 1), 0.0)
        taps_last[...] = total.astype(BF16)[:, :inner]

    for copy in halo_copies:
        copy.wait_recv()

    share = members // halves
    group = 2 if share % 2 == 0 else 1
    fore_copies = {}
    for half in range(halves):
        forecasts = []
        for start in range(half * share, (half + 1) * share, group):
            ids = range(start, start + group)
            own = [state_ref[m].astype(F32) for m in ids]
            stacked = [
                shifted(jnp.concatenate([halo_in[0, m].astype(F32), own[g], halo_in[1, m].astype(F32)], axis=0))
                for g, m in enumerate(ids)
            ]
            hidden = silu(dot(taps_first[...], jnp.concatenate(stacked, axis=1).astype(BF16)))
            for number in range(middle):
                chunk = chunks[number]
                count = hidden.shape[0] // channels - 2
                hidden = hidden.astype(BF16)
                parts = [
                    gathered(dot(taps_middle[number][...], hidden[r * channels : (r + chunk + 2) * channels]), width)
                    for r in range(0, count, chunk)
                ]
                hidden = silu(jnp.concatenate(parts, axis=0))
            change = gathered(dot(taps_last[...], hidden.astype(BF16)), width)
            for g in range(group):
                forecasts.append(own[g] + change[:, g * width : (g + 1) * width])

        per_field = []
        for f in range(fields):
            cube = jnp.stack([v[f * rows : (f + 1) * rows] for v in forecasts], axis=0)
            per_field.append(jnp.transpose(cube, (1, 0, 2)))
        for r in range(rows):
            outbox[half, r] = jnp.concatenate([cube[r] for cube in per_field], axis=0).astype(BF16)

        for s in (0, 2, 1):
            for i in range(n_member):
                if s == 1 and i == 0:
                    continue
                target = member_at(i)
                copy = pltpu.make_async_remote_copy(
                    src_ref=outbox.at[half, target],
                    dst_ref=inbox.at[s, half, me],
                    send_sem=fore_send.at[s, half, i],
                    recv_sem=fore_recv.at[s, half, i],
                    device_id=(target, tile_at(1 - s)),
                    device_id_type=MESH,
                )
                copy.start()
                fore_copies[s, half, i] = copy
        inbox[1, half, me] = outbox[half, me]

    read = rows_ref[...]
    spot = lax.broadcasted_iota(jnp.int32, (span, read.shape[1]), 0)
    for s in range(3):
        onehot[s] = jnp.where(spot == read - s * span, 1.0, 0.0).astype(BF16)
    obs_weight = jnp.exp(-0.25 * class_ref[...].astype(F32)) / variance_ref[...]
    eye_row = lax.broadcasted_iota(jnp.int32, (ensemble, 2 * ensemble), 0)
    eye_col = lax.broadcasted_iota(jnp.int32, (ensemble, 2 * ensemble), 1)
    identity = jnp.where((eye_row == eye_col) | (eye_row + ensemble == eye_col), 1.0, 0.0).astype(F32)

    def neighbour(s):
        blocks = [inbox[s, half, k].astype(F32) for k in range(n_member) for half in range(halves)]
        columns = [
            jnp.concatenate([b[f * share : (f + 1) * share] for b in blocks], axis=0) for f in range(fields)
        ]
        return jnp.concatenate(columns, axis=1)

    obs_ens = None
    back = None
    for s in (1, 0, 2):
        for half in range(halves):
            for i in range(n_member):
                if (s, half, i) in fore_copies:
                    fore_copies[s, half, i].wait_recv()
        values = neighbour(s)
        if s == 1:
            back = values
        part = dot(values.astype(BF16), onehot[s])
        obs_ens = part if obs_ens is None else obs_ens + part

    obs_mean = jnp.sum(obs_ens, axis=0, keepdims=True) / ensemble
    obs_anom = obs_ens - obs_mean
    anom_high, anom_low = split(obs_anom)
    heavy_high, heavy_low = split(obs_weight * obs_anom)
    gram = (ensemble - 1.0) * identity + lax.dot_general(
        jnp.concatenate([anom_high, anom_low, anom_high], axis=1),
        jnp.concatenate([jnp.concatenate([heavy_high, heavy_high, heavy_low], axis=1)] * 2, axis=0),
        (((1,), (1,)), ((), ())),
        preferred_element_type=F32,
    )
    residual = jnp.sum(obs_anom * (obs_weight * (observed_ref[...] - obs_mean)), axis=1, keepdims=True)
    norm_scale = jnp.sqrt(0.5 * jnp.sum(gram * gram, keepdims=True))
    iterate_y = gram / norm_scale
    iterate_z = 1.5 * identity - 0.5 * iterate_y
    iterate_y = dot_split(iterate_y, iterate_z)
    for sweep in range(1, NS_ITERS):
        factor = 1.5 * identity - 0.5 * dot_split(iterate_z, iterate_y)
        if sweep + 1 < NS_ITERS:
            iterate_y = dot_split(iterate_y, factor)
        iterate_z = dot_split(factor, iterate_z)
    root_inv = iterate_z / jnp.sqrt(norm_scale)
    back_mean = jnp.sum(back, axis=0, keepdims=True) / ensemble
    back_anom = back - back_mean
    both = dot_split(root_inv, jnp.concatenate([back_anom, jnp.broadcast_to(residual, (ensemble, 128))], axis=1))
    moved, pull = both[:, :span], both[:, span : span + 1]
    shift = back_mean + jnp.sum(pull * moved, axis=0, keepdims=True)
    analysed = shift + (ensemble - 1.0) ** 0.5 * moved

    for k in range(n_member):
        rows_k = analysed[k * members : (k + 1) * members]
        back_out[k] = jnp.concatenate(
            [rows_k[:, f * width : (f + 1) * width] for f in range(fields)], axis=0
        ).astype(BF16)
    back_copies = []
    for i in range(1, n_member):
        target = member_at(i)
        copy = pltpu.make_async_remote_copy(
            src_ref=back_out.at[target],
            dst_ref=back_in.at[me],
            send_sem=back_send.at[i],
            recv_sem=back_recv.at[i],
            device_id=(target, tile),
            device_id_type=MESH,
        )
        copy.start()
        back_copies.append(copy)
    back_in[me] = back_out[me]
    for copy in halo_copies:
        copy.wait_send()
    for copy in fore_copies.values():
        copy.wait_send()
    for copy in back_copies:
        copy.wait_recv()
    landed = [back_in[r].astype(F32) for r in range(rows)]
    per_field = []
    for f in range(fields):
        cube = jnp.stack([v[f * members : (f + 1) * members] for v in landed], axis=0)
        per_field.append(jnp.transpose(cube, (1, 0, 2)))
    for m in range(members):
        out_ref[m] = jnp.concatenate([cube[m] for cube in per_field], axis=0).astype(BF16)
    for copy in back_copies:
        copy.wait_send()


def local(state, first_weight, middle_weight, last_weight, observations, obs_variance, observation_rows, loc_class):
    members, fields, rows, width = state.shape
    channels = first_weight.shape[0]
    middle = middle_weight.shape[0]
    depth = middle + 2
    n_member = lax.axis_size("member")
    n_tile = lax.axis_size("tile")
    assert rows == n_member and n_tile >= 3
    kept = depth
    while fields * kept % 16:
        kept += 1
    assert kept <= rows
    block = fields * rows
    first_rows = rows + 2 * (depth - 1)
    count = 3 * (block + 2 * fields * kept)
    lanes = -(-count // 128) * 128
    obs = observations.shape[2]
    span = fields * width
    spread = jnp.asarray(first_selector(fields, rows, kept, depth, first_rows, lanes), BF16)
    operands = (
        state.reshape(members, block, width),
        spread,
        jnp.transpose(first_weight, (2, 3, 1, 0)).reshape(9, fields, channels),
        jnp.transpose(middle_weight, (0, 3, 4, 1, 2)).reshape(9 * middle, channels, channels),
        jnp.transpose(last_weight, (2, 3, 0, 1)).reshape(9, fields, channels),
        observations[0],
        obs_variance[0],
        observation_rows[0],
        loc_class[0],
    )
    halves = 1
    chunks = []
    for n in range(middle):
        out_rows = rows + 2 * (depth - 2 - n)
        most = max(1, 256 // channels - 2)
        chunks.append(max(c for c in range(1, out_rows + 1) if out_rows % c == 0 and c <= most))
    sizes = (n_member, n_tile, members, fields, rows, width, channels, depth, kept, lanes, halves, chunks)
    vmem = pl.BlockSpec(memory_space=pltpu.VMEM)
    packet = (fields * members, width)
    out = pl.pallas_call(
        functools.partial(kernel, sizes),
        out_shape=pltpu.VMEM((members, block, width), BF16),
        in_specs=[pl.BlockSpec(memory_space=pltpu.HBM)] * len(operands),
        out_specs=vmem,
        scratch_shapes=[
            *[pltpu.VMEM(v.shape, v.dtype) for v in operands],
            pltpu.VMEM((first_rows * channels, count), BF16),
            *[
                pltpu.VMEM((3 * chunks[n] * channels, (chunks[n] + 2) * channels), BF16)
                for n in range(middle)
            ],
            pltpu.VMEM((3 * block, (rows + 2) * channels), BF16),
            pltpu.VMEM((3, span, obs), BF16),
            pltpu.VMEM((2, members, fields * kept, width), BF16),
            pltpu.VMEM((2, members, fields * kept, width), BF16),
            pltpu.VMEM((halves, n_member, fields * members // halves, width), BF16),
            pltpu.VMEM((3, halves, n_member, fields * members // halves, width), BF16),
            pltpu.VMEM((n_member, *packet), BF16),
            pltpu.VMEM((n_member, *packet), BF16),
            pltpu.SemaphoreType.DMA((len(operands),)),
            pltpu.SemaphoreType.DMA((2,)),
            pltpu.SemaphoreType.DMA((2,)),
            pltpu.SemaphoreType.DMA((3, halves, n_member)),
            pltpu.SemaphoreType.DMA((3, halves, n_member)),
            pltpu.SemaphoreType.DMA((n_member,)),
            pltpu.SemaphoreType.DMA((n_member,)),
        ],
        compiler_params=pltpu.CompilerParams(
            collective_id=0, has_side_effects=True, vmem_limit_bytes=60 * 1024 * 1024
        ),
    )(*operands)
    return out.reshape(members, fields, rows, width)


def solution(mesh):
    return jax.shard_map(
        local,
        mesh=mesh,
        in_specs=(
            P("member", None, "tile", None),
            P(),
            P(),
            P(),
            P("tile", "member", None),
            P("tile", "member", None),
            P("tile", "member", None),
            P("tile", "member", None),
        ),
        out_specs=P("member", None, "tile", None),
        check_vma=False,
    )
```

```python
import functools

import jax
import jax.numpy as jnp
import numpy as np
from jax import lax
from jax.experimental import pallas as pl
from jax.experimental.pallas import tpu as pltpu
from jax.sharding import PartitionSpec as P

NS_ITERS = 4
MESH = pl.DeviceIdType.MESH
F32 = jnp.float32
BF16 = jnp.bfloat16


def silu(v):
    half = 0.5 * v
    return half + half * jnp.tanh(half)


def first_selector(fields, rows, kept, halo, out_rows, lanes):
    where = [(f, halo - kept + q) for f in range(fields) for q in range(kept)]
    where += [(f, halo + r) for f in range(fields) for r in range(rows)]
    where += [(f, halo + rows + q) for f in range(fields) for q in range(kept)]
    count = len(where)
    spread = np.zeros((3, 3, fields, out_rows, lanes), np.float32)
    for dx in range(3):
        for k, (f, row) in enumerate(where):
            for r in range(out_rows):
                if 0 <= row - r <= 2:
                    spread[row - r, dx, f, r, dx * count + k] = 1
    return spread.reshape(9 * fields, out_rows * lanes)


def dot(a, b):
    return jnp.dot(a, b, preferred_element_type=F32)


def split(v):
    high = v.astype(BF16)
    return high, (v - high.astype(F32)).astype(BF16)


def dot_split(a_twice, b):
    high, low = split(a_twice)
    size = a_twice.shape[0]
    lane = lax.broadcasted_iota(jnp.int32, a_twice.shape, 1)
    mixed = jnp.where(lane < size, high.astype(F32), low.astype(F32)).astype(BF16)
    b_high, b_low = split(b)
    return dot(jnp.concatenate([mixed, mixed], axis=1), jnp.concatenate([b_high, b_high, b_low, b_low], axis=0))


def shifted(v):
    width = v.shape[1]
    return jnp.concatenate([pltpu.roll(v, 1, 1), v, pltpu.roll(v, width - 1, 1)], axis=0)


def gathered(parts, width):
    third = parts.shape[0] // 3
    sums = []
    for at in range(0, parts.shape[1], width):
        part = parts[:, at : at + width]
        left, right = pltpu.roll(part[:third], 1, 1), pltpu.roll(part[2 * third :], width - 1, 1)
        sums.append(part[third : 2 * third] + left + right)
    return jnp.concatenate(sums, axis=1)


def tap_rows(load, padded):
    lines = []
    for dx in range(3):
        parts = [load(3 * dy + dx) for dy in range(3)]
        filler = jnp.zeros((parts[0].shape[0], padded - 3 * parts[0].shape[1]), F32)
        lines.append(jnp.concatenate([*parts, filler], axis=1))
    return jnp.concatenate(lines, axis=0)


def kernel(sizes, *refs):
    n_member, n_tile, members, fields, rows, width, channels, depth, kept, lanes, halves, chunks = sizes
    middle = depth - 2
    sources, out_ref, refs = refs[:9], refs[9], refs[10:]
    fetched, refs = refs[:9], refs[9:]
    (
        state_ref, spread_ref, first_ref, middle_ref, last_ref, observed_ref, variance_ref, rows_ref, class_ref,
    ) = fetched
    taps_first, taps_middle, refs = refs[0], refs[1 : 1 + middle], refs[1 + middle :]
    (
        taps_last, onehot, halo_out, halo_in, obs_all, outbox, inbox, sums_out, sums_in, back_out, back_in,
        fetch_sem, halo_send, halo_recv, obs_send, obs_recv, fore_send, fore_recv, sums_send, sums_recv,
        back_send, back_recv,
    ) = refs
    fetches = [
        pltpu.make_async_copy(source, target, fetch_sem.at[n])
        for n, (source, target) in enumerate(zip(sources, fetched))
    ]
    fetches[0].start()
    me = lax.axis_index("member")
    tile = lax.axis_index("tile")
    block = fields * rows
    ensemble = n_member * members
    span = fields * width

    def wrapped(index, count):
        index = jnp.where(index >= count, index - count, index)
        return jnp.where(index < 0, index + count, index)

    def tile_at(shift):
        return wrapped(tile + shift, n_tile) if shift else tile

    def member_at(shift):
        return wrapped(me + shift, n_member) if shift else me

    barrier = pltpu.get_barrier_semaphore()
    peers = [(0, 1), (0, -1)] + [(i, 0) for i in range(1, n_member)]
    for i, d in peers:
        pl.semaphore_signal(barrier, inc=1, device_id=(member_at(i), tile_at(d)), device_id_type=MESH)

    for fetch in fetches[1:]:
        fetch.start()
    fetches[0].wait()
    for m in range(members):
        whole = state_ref[m].astype(F32)
        each = [whole[f * rows : (f + 1) * rows] for f in range(fields)]
        halo_out[0, m] = jnp.concatenate([v[rows - kept :] for v in each], axis=0).astype(BF16)
        halo_out[1, m] = jnp.concatenate([v[:kept] for v in each], axis=0).astype(BF16)
    pl.semaphore_wait(barrier, len(peers))
    halo_copies = []
    for side, d in ((0, 1), (1, -1)):
        copy = pltpu.make_async_remote_copy(
            src_ref=halo_out.at[side],
            dst_ref=halo_in.at[side],
            send_sem=halo_send.at[side],
            recv_sem=halo_recv.at[side],
            device_id=(me, tile_at(d)),
            device_id_type=MESH,
        )
        copy.start()
        halo_copies.append(copy)

    for fetch in fetches[1:]:
        fetch.wait()
    obs_count = rows_ref.shape[1]
    obs_weight = jnp.exp(-0.25 * class_ref[...].astype(F32)) / variance_ref[...]
    obs_all[1] = jnp.concatenate(
        [rows_ref[...].astype(F32), obs_weight, observed_ref[...], jnp.zeros((5, obs_count), F32)], axis=0
    )
    obs_copies = []
    for side, d in ((0, 1), (2, -1)):
        copy = pltpu.make_async_remote_copy(
            src_ref=obs_all.at[1],
            dst_ref=obs_all.at[side],
            send_sem=obs_send.at[side],
            recv_sem=obs_recv.at[side],
            device_id=(me, tile_at(d)),
            device_id_type=MESH,
        )
        copy.start()
        obs_copies.append(copy)

    with jax.named_scope("taps"):
        first_taps = jnp.concatenate([first_ref[n].astype(F32) for n in range(9)], axis=0).astype(BF16)
        wide = lax.dot_general(
            first_taps, spread_ref[...], (((0,), (0,)), ((), ())), preferred_element_type=F32
        ).astype(BF16)
        first_rows = rows + 2 * (depth - 1)
        count = taps_first.shape[1]
        for r in range(first_rows):
            taps_first[r * channels : (r + 1) * channels, :] = wide[:, r * lanes : r * lanes + count]
        for number in range(middle):
            chunk = chunks[number]
            inner = (chunk + 2) * channels
            padded = -(-inner // 128) * 128
            base = tap_rows(lambda n: middle_ref[9 * number + n].astype(F32), padded)
            for r in range(chunk):
                moved = (pltpu.roll(base, r * channels, 1) if r else base).astype(BF16)
                for dx in range(3):
                    at = (dx * chunk + r) * channels
                    taps_middle[number][at : at + channels, :] = moved[dx * channels : (dx + 1) * channels, :inner]
        inner = (rows + 2) * channels
        padded = -(-inner // 128) * 128
        base = tap_rows(lambda n: last_ref[n].astype(F32), padded)
        base = jnp.broadcast_to(base[:, None, :], (base.shape[0], rows, padded)).reshape(-1, padded)
        row_of = lax.rem(lax.broadcasted_iota(jnp.int32, base.shape, 0), rows)
        total = jnp.where(row_of == 0, base, 0.0)
        for r in range(1, rows):
            total = total + jnp.where(row_of == r, pltpu.roll(base, r * channels, 1), 0.0)
        taps_last[...] = total.astype(BF16)[:, :inner]

    for copy in halo_copies:
        copy.wait_recv()

    share = members // halves
    group = 2 if share % 2 == 0 else 1
    fore_copies = {}
    for half in range(halves):
        forecasts = []
        for start in range(half * share, (half + 1) * share, group):
            ids = range(start, start + group)
            own = [state_ref[m].astype(F32) for m in ids]
            stacked = [
                shifted(jnp.concatenate([halo_in[0, m].astype(F32), own[g], halo_in[1, m].astype(F32)], axis=0))
                for g, m in enumerate(ids)
            ]
            hidden = silu(dot(taps_first[...], jnp.concatenate(stacked, axis=1).astype(BF16)))
            for number in range(middle):
                chunk = chunks[number]
                count = hidden.shape[0] // channels - 2
                hidden = hidden.astype(BF16)
                parts = [
                    gathered(dot(taps_middle[number][...], hidden[r * channels : (r + chunk + 2) * channels]), width)
                    for r in range(0, count, chunk)
                ]
                hidden = silu(jnp.concatenate(parts, axis=0))
            change = gathered(dot(taps_last[...], hidden.astype(BF16)), width)
            for g in range(group):
                forecasts.append(own[g] + change[:, g * width : (g + 1) * width])

        per_field = []
        for f in range(fields):
            cube = jnp.stack([v[f * rows : (f + 1) * rows] for v in forecasts], axis=0)
            per_field.append(jnp.transpose(cube, (1, 0, 2)))
        for r in range(rows):
            outbox[half, r] = jnp.concatenate([cube[r] for cube in per_field], axis=0).astype(BF16)

        for i in range(1, n_member):
            target = member_at(i)
            copy = pltpu.make_async_remote_copy(
                src_ref=outbox.at[half, target],
                dst_ref=inbox.at[half, me],
                send_sem=fore_send.at[half, i],
                recv_sem=fore_recv.at[half, i],
                device_id=(target, tile),
                device_id_type=MESH,
            )
            copy.start()
            fore_copies[half, i] = copy
        inbox[half, me] = outbox[half, me]

    for copy in obs_copies:
        copy.wait_recv()
    spot = lax.broadcasted_iota(jnp.int32, (span, obs_count), 0).astype(F32)
    for slot in range(3):
        read = obs_all[slot][0:1] - float((2 - slot) * span)
        onehot[slot] = jnp.where(spot == read, 1.0, 0.0).astype(BF16)
    eye_row = lax.broadcasted_iota(jnp.int32, (ensemble, 2 * ensemble), 0)
    eye_col = lax.broadcasted_iota(jnp.int32, (ensemble, 2 * ensemble), 1)
    identity = jnp.where((eye_row == eye_col) | (eye_row + ensemble == eye_col), 1.0, 0.0).astype(F32)

    left = eye_col < ensemble

    for copy in fore_copies.values():
        copy.wait_recv()
    blocks = [inbox[half, k].astype(F32) for k in range(n_member) for half in range(halves)]
    columns = [jnp.concatenate([b[f * share : (f + 1) * share] for b in blocks], axis=0) for f in range(fields)]
    back = jnp.concatenate(columns, axis=1)
    back_low = back.astype(BF16)

    def partial_sums(slot):
        given = obs_all[slot]
        obs_ens = dot(back_low, onehot[slot])
        obs_mean = jnp.sum(obs_ens, axis=0, keepdims=True) / ensemble
        obs_anom = obs_ens - obs_mean
        misfit = jnp.broadcast_to(given[2:3] - obs_mean, (8, obs_count))
        high, low = split(jnp.concatenate([obs_anom, misfit], axis=0))
        heavy_high, heavy_low = split(given[1:2] * obs_anom)
        heavy = jnp.concatenate([heavy_high, heavy_high, heavy_low], axis=1)
        total = lax.dot_general(
            jnp.concatenate([high, low, high], axis=1),
            jnp.concatenate([heavy, heavy], axis=0),
            (((1,), (1,)), ((), ())),
            preferred_element_type=F32,
        )
        middle_row = ensemble // 2
        folded = jnp.where(left[:middle_row], total[:middle_row], total[middle_row:ensemble])
        return jnp.concatenate([folded, total[ensemble:]], axis=0)

    sums_copies = []
    for side, d in ((0, -1), (2, 1)):
        sums_out[side // 2] = partial_sums(side)
        copy = pltpu.make_async_remote_copy(
            src_ref=sums_out.at[side // 2],
            dst_ref=sums_in.at[side // 2],
            send_sem=sums_send.at[side // 2],
            recv_sem=sums_recv.at[side // 2],
            device_id=(me, tile_at(d)),
            device_id_type=MESH,
        )
        copy.start()
        sums_copies.append(copy)
    sums = partial_sums(1)
    back_mean = jnp.sum(back, axis=0, keepdims=True) / ensemble
    back_anom = back - back_mean
    for copy in sums_copies:
        copy.wait_recv()
    sums = sums + sums_in[0] + sums_in[1]
    middle_row = ensemble // 2
    folded, residual = sums[:middle_row], sums[middle_row : middle_row + 1]
    turned = pltpu.roll(folded, ensemble, 1)
    gram = (ensemble - 1.0) * identity + jnp.concatenate(
        [jnp.where(left[:middle_row], folded, turned), jnp.where(left[:middle_row], turned, folded)], axis=0
    )
    norm_scale = jnp.sqrt(0.5 * jnp.sum(gram * gram, keepdims=True))
    iterate_y = gram / norm_scale
    iterate_z = 1.5 * identity - 0.5 * iterate_y
    iterate_y = dot_split(iterate_y, iterate_z)
    for sweep in range(1, NS_ITERS):
        factor = 1.5 * identity - 0.5 * dot_split(iterate_z, iterate_y)
        if sweep + 1 < NS_ITERS:
            iterate_y = dot_split(iterate_y, factor)
        iterate_z = dot_split(factor, iterate_z)
    root_inv = iterate_z / jnp.sqrt(norm_scale)
    moved = dot_split(root_inv, back_anom)
    pull = 0.5 * jnp.sum(root_inv * residual, axis=1, keepdims=True)
    shift = back_mean + jnp.sum(pull * moved, axis=0, keepdims=True)
    analysed = shift + (ensemble - 1.0) ** 0.5 * moved

    for k in range(n_member):
        rows_k = analysed[k * members : (k + 1) * members]
        back_out[k] = jnp.concatenate(
            [rows_k[:, f * width : (f + 1) * width] for f in range(fields)], axis=0
        ).astype(BF16)
    back_copies = []
    for i in range(1, n_member):
        target = member_at(i)
        copy = pltpu.make_async_remote_copy(
            src_ref=back_out.at[target],
            dst_ref=back_in.at[me],
            send_sem=back_send.at[i],
            recv_sem=back_recv.at[i],
            device_id=(target, tile),
            device_id_type=MESH,
        )
        copy.start()
        back_copies.append(copy)
    back_in[me] = back_out[me]
    for copy in halo_copies:
        copy.wait_send()
    for copy in (*obs_copies, *fore_copies.values(), *sums_copies):
        copy.wait_send()
    for copy in back_copies:
        copy.wait_recv()
    landed = [back_in[r].astype(F32) for r in range(rows)]
    per_field = []
    for f in range(fields):
        cube = jnp.stack([v[f * members : (f + 1) * members] for v in landed], axis=0)
        per_field.append(jnp.transpose(cube, (1, 0, 2)))
    for m in range(members):
        out_ref[m] = jnp.concatenate([cube[m] for cube in per_field], axis=0).astype(BF16)
    for copy in back_copies:
        copy.wait_send()


def local(state, first_weight, middle_weight, last_weight, observations, obs_variance, observation_rows, loc_class):
    members, fields, rows, width = state.shape
    channels = first_weight.shape[0]
    middle = middle_weight.shape[0]
    depth = middle + 2
    n_member = lax.axis_size("member")
    n_tile = lax.axis_size("tile")
    assert rows == n_member and n_tile >= 3
    kept = depth
    while fields * kept % 16:
        kept += 1
    assert kept <= rows
    ensemble = n_member * members
    block = fields * rows
    first_rows = rows + 2 * (depth - 1)
    count = 3 * (block + 2 * fields * kept)
    lanes = -(-count // 128) * 128
    obs = observations.shape[2]
    span = fields * width
    spread = jnp.asarray(first_selector(fields, rows, kept, depth, first_rows, lanes), BF16)
    operands = (
        state.reshape(members, block, width),
        spread,
        jnp.transpose(first_weight, (2, 3, 1, 0)).reshape(9, fields, channels),
        jnp.transpose(middle_weight, (0, 3, 4, 1, 2)).reshape(9 * middle, channels, channels),
        jnp.transpose(last_weight, (2, 3, 0, 1)).reshape(9, fields, channels),
        observations[0],
        obs_variance[0],
        observation_rows[0],
        loc_class[0],
    )
    halves = 1
    chunks = []
    for n in range(middle):
        out_rows = rows + 2 * (depth - 2 - n)
        most = max(1, 256 // channels - 2)
        chunks.append(max(c for c in range(1, out_rows + 1) if out_rows % c == 0 and c <= most))
    sizes = (n_member, n_tile, members, fields, rows, width, channels, depth, kept, lanes, halves, chunks)
    vmem = pl.BlockSpec(memory_space=pltpu.VMEM)
    packet = (fields * members, width)
    out = pl.pallas_call(
        functools.partial(kernel, sizes),
        out_shape=pltpu.VMEM((members, block, width), BF16),
        in_specs=[pl.BlockSpec(memory_space=pltpu.HBM)] * len(operands),
        out_specs=vmem,
        scratch_shapes=[
            *[pltpu.VMEM(v.shape, v.dtype) for v in operands],
            pltpu.VMEM((first_rows * channels, count), BF16),
            *[
                pltpu.VMEM((3 * chunks[n] * channels, (chunks[n] + 2) * channels), BF16)
                for n in range(middle)
            ],
            pltpu.VMEM((3 * block, (rows + 2) * channels), BF16),
            pltpu.VMEM((3, span, obs), BF16),
            pltpu.VMEM((2, members, fields * kept, width), BF16),
            pltpu.VMEM((2, members, fields * kept, width), BF16),
            pltpu.VMEM((3, 8, obs), F32),
            pltpu.VMEM((halves, n_member, fields * members // halves, width), BF16),
            pltpu.VMEM((halves, n_member, fields * members // halves, width), BF16),
            pltpu.VMEM((2, ensemble // 2 + 8, 2 * ensemble), F32),
            pltpu.VMEM((2, ensemble // 2 + 8, 2 * ensemble), F32),
            pltpu.VMEM((n_member, *packet), BF16),
            pltpu.VMEM((n_member, *packet), BF16),
            pltpu.SemaphoreType.DMA((len(operands),)),
            pltpu.SemaphoreType.DMA((2,)),
            pltpu.SemaphoreType.DMA((2,)),
            pltpu.SemaphoreType.DMA((3,)),
            pltpu.SemaphoreType.DMA((3,)),
            pltpu.SemaphoreType.DMA((halves, n_member)),
            pltpu.SemaphoreType.DMA((halves, n_member)),
            pltpu.SemaphoreType.DMA((2,)),
            pltpu.SemaphoreType.DMA((2,)),
            pltpu.SemaphoreType.DMA((n_member,)),
            pltpu.SemaphoreType.DMA((n_member,)),
        ],
        compiler_params=pltpu.CompilerParams(
            collective_id=0, has_side_effects=True, vmem_limit_bytes=60 * 1024 * 1024
        ),
    )(*operands)
    return out.reshape(members, fields, rows, width)


def solution(mesh):
    return jax.shard_map(
        local,
        mesh=mesh,
        in_specs=(
            P("member", None, "tile", None),
            P(),
            P(),
            P(),
            P("tile", "member", None),
            P("tile", "member", None),
            P("tile", "member", None),
            P("tile", "member", None),
        ),
        out_specs=P("member", None, "tile", None),
        check_vma=False,
    )
```

```python
import functools

import jax
import jax.numpy as jnp
import numpy as np
from jax import lax
from jax.experimental import pallas as pl
from jax.experimental.pallas import tpu as pltpu
from jax.sharding import PartitionSpec as P

NS_ITERS = 4
MESH = pl.DeviceIdType.MESH
F32 = jnp.float32
BF16 = jnp.bfloat16


def silu(v):
    half = 0.5 * v
    return half + half * jnp.tanh(half)


def first_selector(fields, rows, kept, halo, out_rows, lanes):
    where = [(f, halo - kept + q) for f in range(fields) for q in range(kept)]
    where += [(f, halo + r) for f in range(fields) for r in range(rows)]
    where += [(f, halo + rows + q) for f in range(fields) for q in range(kept)]
    count = len(where)
    spread = np.zeros((3, 3, fields, out_rows, lanes), np.float32)
    for dx in range(3):
        for k, (f, row) in enumerate(where):
            for r in range(out_rows):
                if 0 <= row - r <= 2:
                    spread[row - r, dx, f, r, dx * count + k] = 1
    return spread.reshape(9 * fields, out_rows * lanes)


def dot(a, b):
    return jnp.dot(a, b, preferred_element_type=F32)


def split(v):
    high = v.astype(BF16)
    return high, (v - high.astype(F32)).astype(BF16)


def dot_split(a_twice, b):
    high, low = split(a_twice)
    size = a_twice.shape[0]
    lane = lax.broadcasted_iota(jnp.int32, a_twice.shape, 1)
    mixed = jnp.where(lane < size, high.astype(F32), low.astype(F32)).astype(BF16)
    b_high, b_low = split(b)
    return dot(jnp.concatenate([mixed, mixed], axis=1), jnp.concatenate([b_high, b_high, b_low, b_low], axis=0))


def shifted(v):
    width = v.shape[1]
    return jnp.concatenate([pltpu.roll(v, 1, 1), v, pltpu.roll(v, width - 1, 1)], axis=0)


def gathered(parts, width):
    third = parts.shape[0] // 3
    sums = []
    for at in range(0, parts.shape[1], width):
        part = parts[:, at : at + width]
        left, right = pltpu.roll(part[:third], 1, 1), pltpu.roll(part[2 * third :], width - 1, 1)
        sums.append(part[third : 2 * third] + left + right)
    return jnp.concatenate(sums, axis=1)


def tap_rows(load, padded):
    lines = []
    for dx in range(3):
        parts = [load(3 * dy + dx) for dy in range(3)]
        filler = jnp.zeros((parts[0].shape[0], padded - 3 * parts[0].shape[1]), F32)
        lines.append(jnp.concatenate([*parts, filler], axis=1))
    return jnp.concatenate(lines, axis=0)


def kernel(sizes, *refs):
    n_member, n_tile, members, fields, rows, width, channels, depth, kept, lanes, halves, chunks = sizes
    middle = depth - 2
    sources, out_ref, refs = refs[:9], refs[9], refs[10:]
    fetched, refs = refs[:9], refs[9:]
    (
        state_ref, spread_ref, first_ref, middle_ref, last_ref, observed_ref, variance_ref, rows_ref, class_ref,
    ) = fetched
    taps_first, taps_middle, refs = refs[0], refs[1 : 1 + middle], refs[1 + middle :]
    (
        taps_last, mixed, onehot, halo_out, halo_in, outbox, inbox, back_out, back_in, fetch_sem,
        halo_send, halo_recv, fore_send, fore_recv, back_send, back_recv,
    ) = refs
    fetches = [
        pltpu.make_async_copy(source, target, fetch_sem.at[n])
        for n, (source, target) in enumerate(zip(sources, fetched))
    ]
    fetches[0].start()
    me = lax.axis_index("member")
    tile = lax.axis_index("tile")
    block = fields * rows
    ensemble = n_member * members
    span = fields * width

    def wrapped(index, count):
        index = jnp.where(index >= count, index - count, index)
        return jnp.where(index < 0, index + count, index)

    def tile_at(shift):
        return wrapped(tile + shift, n_tile) if shift else tile

    def member_at(shift):
        return wrapped(me + shift, n_member) if shift else me

    barrier = pltpu.get_barrier_semaphore()
    peers = [(i, d) for d in (1, -1, 0) for i in range(n_member) if (i, d) != (0, 0)]
    for i, d in peers:
        pl.semaphore_signal(barrier, inc=1, device_id=(member_at(i), tile_at(d)), device_id_type=MESH)

    for fetch in fetches[1:]:
        fetch.start()
    fetches[0].wait()
    for m in range(members):
        whole = state_ref[m].astype(F32)
        each = [whole[f * rows : (f + 1) * rows] for f in range(fields)]
        halo_out[0, m] = jnp.concatenate([v[rows - kept :] for v in each], axis=0).astype(BF16)
        halo_out[1, m] = jnp.concatenate([v[:kept] for v in each], axis=0).astype(BF16)
    pl.semaphore_wait(barrier, len(peers))
    halo_copies = []
    for side, d in ((0, 1), (1, -1)):
        copy = pltpu.make_async_remote_copy(
            src_ref=halo_out.at[side],
            dst_ref=halo_in.at[side],
            send_sem=halo_send.at[side],
            recv_sem=halo_recv.at[side],
            device_id=(me, tile_at(d)),
            device_id_type=MESH,
        )
        copy.start()
        halo_copies.append(copy)

    with jax.named_scope("taps"):
        for fetch in fetches[1:]:
            fetch.wait()
        first_taps = jnp.concatenate([first_ref[n].astype(F32) for n in range(9)], axis=0).astype(BF16)
        wide = lax.dot_general(
            first_taps, spread_ref[...], (((0,), (0,)), ((), ())), preferred_element_type=F32
        ).astype(BF16)
        first_rows = rows + 2 * (depth - 1)
        count = taps_first.shape[1]
        for r in range(first_rows):
            taps_first[r * channels : (r + 1) * channels, :] = wide[:, r * lanes : r * lanes + count]
        for number in range(middle):
            chunk = chunks[number]
            inner = (chunk + 2) * channels
            padded = -(-inner // 128) * 128
            base = tap_rows(lambda n: middle_ref[9 * number + n].astype(F32), padded)
            for r in range(chunk):
                moved = (pltpu.roll(base, r * channels, 1) if r else base).astype(BF16)
                for dx in range(3):
                    at = (dx * chunk + r) * channels
                    taps_middle[number][at : at + channels, :] = moved[dx * channels : (dx + 1) * channels, :inner]
        inner = (rows + 2) * channels
        padded = -(-inner // 128) * 128
        base = tap_rows(lambda n: last_ref[n].astype(F32), padded)
        base = jnp.broadcast_to(base[:, None, :], (base.shape[0], rows, padded)).reshape(-1, padded)
        row_of = lax.rem(lax.broadcasted_iota(jnp.int32, base.shape, 0), rows)
        total = jnp.where(row_of == 0, base, 0.0)
        for r in range(1, rows):
            total = total + jnp.where(row_of == r, pltpu.roll(base, r * channels, 1), 0.0)
        taps_last[...] = total.astype(BF16)[:, :inner]

    for copy in halo_copies:
        copy.wait_recv()

    share = members // halves
    group = 2 if share % 2 == 0 else 1
    fore_copies = {}
    for half in range(halves):
        groups = [range(start, start + group) for start in range(half * share, (half + 1) * share, group)]
        hidden = []
        for ids in groups:
            stacked = [
                shifted(jnp.concatenate([halo_in[0, m], state_ref[m], halo_in[1, m]], axis=0).astype(F32))
                for m in ids
            ]
            hidden.append(silu(dot(taps_first[...], jnp.concatenate(stacked, axis=1).astype(BF16))).astype(BF16))
        for number in range(middle):
            chunk = chunks[number]
            count = hidden[0].shape[0] // channels - 2
            latest = []
            for before in hidden:
                parts = []
                for r in range(0, count, chunk):
                    product = dot(taps_middle[number][...], before[r * channels : (r + chunk + 2) * channels])
                    parts.append(silu(gathered(product, width)).astype(BF16))
                latest.append(jnp.concatenate(parts, axis=0))
            hidden = latest
        for ids, before in zip(groups, hidden):
            change = gathered(dot(taps_last[...], before), width)
            for g, m in enumerate(ids):
                mixed[m * block : (m + 1) * block, :] = (
                    state_ref[m].astype(F32) + change[:, g * width : (g + 1) * width]
                )

        for r in range(rows):
            outbox[half, r] = jnp.concatenate(
                [mixed[pl.ds(half * share * block + f * rows + r, share, stride=block), :] for f in range(fields)],
                axis=0,
            ).astype(BF16)

        for s in (0, 2, 1):
            for i in range(n_member):
                if s == 1 and i == 0:
                    continue
                target = member_at(i)
                copy = pltpu.make_async_remote_copy(
                    src_ref=outbox.at[half, target],
                    dst_ref=inbox.at[s, half, me],
                    send_sem=fore_send.at[s, half, i],
                    recv_sem=fore_recv.at[s, half, i],
                    device_id=(target, tile_at(1 - s)),
                    device_id_type=MESH,
                )
                copy.start()
                fore_copies[s, half, i] = copy
        inbox[1, half, me] = outbox[half, me]

    read = rows_ref[...]
    spot = lax.broadcasted_iota(jnp.int32, (span, read.shape[1]), 0)
    for s in range(3):
        onehot[s] = jnp.where(spot == read - s * span, 1.0, 0.0).astype(BF16)
    obs_weight = jnp.exp(-0.25 * class_ref[...].astype(F32)) / variance_ref[...]
    eye_row = lax.broadcasted_iota(jnp.int32, (ensemble, 2 * ensemble), 0)
    eye_col = lax.broadcasted_iota(jnp.int32, (ensemble, 2 * ensemble), 1)
    identity = jnp.where((eye_row == eye_col) | (eye_row + ensemble == eye_col), 1.0, 0.0).astype(F32)

    def neighbour(s):
        blocks = [inbox[s, half, k].astype(F32) for k in range(n_member) for half in range(halves)]
        columns = [
            jnp.concatenate([b[f * share : (f + 1) * share] for b in blocks], axis=0) for f in range(fields)
        ]
        return jnp.concatenate(columns, axis=1)

    obs_ens = None
    back = None
    for s in (1, 0, 2):
        for half in range(halves):
            for i in range(n_member):
                if (s, half, i) in fore_copies:
                    fore_copies[s, half, i].wait_recv()
        values = neighbour(s)
        if s == 1:
            back = values
        part = dot(values.astype(BF16), onehot[s])
        obs_ens = part if obs_ens is None else obs_ens + part

    obs_mean = jnp.sum(obs_ens, axis=0, keepdims=True) / ensemble
    obs_anom = obs_ens - obs_mean
    anom_high, anom_low = split(obs_anom)
    heavy_high, heavy_low = split(obs_weight * obs_anom)
    gram = (ensemble - 1.0) * identity + lax.dot_general(
        jnp.concatenate([anom_high, anom_low, anom_high], axis=1),
        jnp.concatenate([jnp.concatenate([heavy_high, heavy_high, heavy_low], axis=1)] * 2, axis=0),
        (((1,), (1,)), ((), ())),
        preferred_element_type=F32,
    )
    residual = jnp.sum(obs_anom * (obs_weight * (observed_ref[...] - obs_mean)), axis=1, keepdims=True)
    norm_scale = jnp.sqrt(0.5 * jnp.sum(gram * gram, keepdims=True))
    iterate_y = gram / norm_scale
    iterate_z = 1.5 * identity - 0.5 * iterate_y
    iterate_y = dot_split(iterate_y, iterate_z)
    for sweep in range(1, NS_ITERS):
        factor = 1.5 * identity - 0.5 * dot_split(iterate_z, iterate_y)
        if sweep + 1 < NS_ITERS:
            iterate_y = dot_split(iterate_y, factor)
        iterate_z = dot_split(factor, iterate_z)
    root_inv = iterate_z / jnp.sqrt(norm_scale)
    back_mean = jnp.sum(back, axis=0, keepdims=True) / ensemble
    back_anom = back - back_mean
    both = dot_split(root_inv, jnp.concatenate([back_anom, jnp.broadcast_to(residual, (ensemble, 128))], axis=1))
    moved, pull = both[:, :span], both[:, span : span + 1]
    shift = back_mean + jnp.sum(pull * moved, axis=0, keepdims=True)
    analysed = shift + (ensemble - 1.0) ** 0.5 * moved

    for k in range(n_member):
        rows_k = analysed[k * members : (k + 1) * members]
        back_out[k] = jnp.concatenate(
            [rows_k[:, f * width : (f + 1) * width] for f in range(fields)], axis=0
        ).astype(BF16)
    back_copies = []
    for i in range(1, n_member):
        target = member_at(i)
        copy = pltpu.make_async_remote_copy(
            src_ref=back_out.at[target],
            dst_ref=back_in.at[me],
            send_sem=back_send.at[i],
            recv_sem=back_recv.at[i],
            device_id=(target, tile),
            device_id_type=MESH,
        )
        copy.start()
        back_copies.append(copy)
    back_in[me] = back_out[me]
    for copy in halo_copies:
        copy.wait_send()
    for copy in fore_copies.values():
        copy.wait_send()
    for copy in back_copies:
        copy.wait_recv()
    pack = fields * members
    for r in range(rows):
        mixed[r * pack : (r + 1) * pack, :] = back_in[r].astype(F32)
    for m in range(members):
        out_ref[m] = jnp.concatenate(
            [mixed[pl.ds(f * members + m, rows, stride=pack), :] for f in range(fields)], axis=0
        ).astype(BF16)
    for copy in back_copies:
        copy.wait_send()


def local(state, first_weight, middle_weight, last_weight, observations, obs_variance, observation_rows, loc_class):
    members, fields, rows, width = state.shape
    channels = first_weight.shape[0]
    middle = middle_weight.shape[0]
    depth = middle + 2
    n_member = lax.axis_size("member")
    n_tile = lax.axis_size("tile")
    assert rows == n_member and n_tile >= 3
    kept = depth
    while fields * kept % 16:
        kept += 1
    assert kept <= rows
    block = fields * rows
    first_rows = rows + 2 * (depth - 1)
    count = 3 * (block + 2 * fields * kept)
    lanes = -(-count // 128) * 128
    obs = observations.shape[2]
    span = fields * width
    spread = jnp.asarray(first_selector(fields, rows, kept, depth, first_rows, lanes), BF16)
    operands = (
        state.reshape(members, block, width),
        spread,
        jnp.transpose(first_weight, (2, 3, 1, 0)).reshape(9, fields, channels),
        jnp.transpose(middle_weight, (0, 3, 4, 1, 2)).reshape(9 * middle, channels, channels),
        jnp.transpose(last_weight, (2, 3, 0, 1)).reshape(9, fields, channels),
        observations[0],
        obs_variance[0],
        observation_rows[0],
        loc_class[0],
    )
    halves = 1
    chunks = []
    for n in range(middle):
        out_rows = rows + 2 * (depth - 2 - n)
        most = max(1, 256 // channels - 2)
        chunks.append(max(c for c in range(1, out_rows + 1) if out_rows % c == 0 and c <= most))
    sizes = (n_member, n_tile, members, fields, rows, width, channels, depth, kept, lanes, halves, chunks)
    vmem = pl.BlockSpec(memory_space=pltpu.VMEM)
    packet = (fields * members, width)
    out = pl.pallas_call(
        functools.partial(kernel, sizes),
        out_shape=pltpu.VMEM((members, block, width), BF16),
        in_specs=[pl.BlockSpec(memory_space=pltpu.HBM)] * len(operands),
        out_specs=vmem,
        scratch_shapes=[
            *[pltpu.VMEM(v.shape, v.dtype) for v in operands],
            pltpu.VMEM((first_rows * channels, count), BF16),
            *[
                pltpu.VMEM((3 * chunks[n] * channels, (chunks[n] + 2) * channels), BF16)
                for n in range(middle)
            ],
            pltpu.VMEM((3 * block, (rows + 2) * channels), BF16),
            pltpu.VMEM((members * block, width), F32),
            pltpu.VMEM((3, span, obs), BF16),
            pltpu.VMEM((2, members, fields * kept, width), BF16),
            pltpu.VMEM((2, members, fields * kept, width), BF16),
            pltpu.VMEM((halves, n_member, fields * members // halves, width), BF16),
            pltpu.VMEM((3, halves, n_member, fields * members // halves, width), BF16),
            pltpu.VMEM((n_member, *packet), BF16),
            pltpu.VMEM((n_member, *packet), BF16),
            pltpu.SemaphoreType.DMA((len(operands),)),
            pltpu.SemaphoreType.DMA((2,)),
            pltpu.SemaphoreType.DMA((2,)),
            pltpu.SemaphoreType.DMA((3, halves, n_member)),
            pltpu.SemaphoreType.DMA((3, halves, n_member)),
            pltpu.SemaphoreType.DMA((n_member,)),
            pltpu.SemaphoreType.DMA((n_member,)),
        ],
        compiler_params=pltpu.CompilerParams(
            collective_id=0, has_side_effects=True, vmem_limit_bytes=60 * 1024 * 1024
        ),
    )(*operands)
    return out.reshape(members, fields, rows, width)


def solution(mesh):
    return jax.shard_map(
        local,
        mesh=mesh,
        in_specs=(
            P("member", None, "tile", None),
            P(),
            P(),
            P(),
            P("tile", "member", None),
            P("tile", "member", None),
            P("tile", "member", None),
            P("tile", "member", None),
        ),
        out_specs=P("member", None, "tile", None),
        check_vma=False,
    )
```

```python
import functools

import jax
import jax.numpy as jnp
import numpy as np
from jax import lax
from jax.experimental import pallas as pl
from jax.experimental.pallas import tpu as pltpu
from jax.sharding import PartitionSpec as P

NS_ITERS = 4
MESH = pl.DeviceIdType.MESH
F32 = jnp.float32
BF16 = jnp.bfloat16


def silu(v):
    half = 0.5 * v
    return half + half * jnp.tanh(half)


def first_selector(fields, where, out_rows, lanes):
    spread = np.zeros((3, 3, fields, len(out_rows), lanes), np.float32)
    for dx in range(3):
        for k, (f, row) in enumerate(where):
            for n, r in enumerate(out_rows):
                if 0 <= row - r <= 2:
                    spread[row - r, dx, f, n, dx * len(where) + k] = 1
    return spread.reshape(9 * fields, len(out_rows) * lanes)


def middle_layer(taps, hidden, chunk, channels, width):
    count = hidden.shape[0] // channels - 2
    parts = [
        silu(gathered(dot(taps, hidden[r * channels : (r + chunk + 2) * channels]), width)).astype(BF16)
        for r in range(0, count, chunk)
    ]
    return jnp.concatenate(parts, axis=0)


def spread_middle(taps, base, chunk, channels):
    inner = (chunk + 2) * channels
    for r in range(chunk):
        moved = (pltpu.roll(base, r * channels, 1) if r else base).astype(BF16)
        for dx in range(3):
            at = (dx * chunk + r) * channels
            taps[at : at + channels, :] = moved[dx * channels : (dx + 1) * channels, :inner]


def dot(a, b):
    return jnp.dot(a, b, preferred_element_type=F32)


def split(v):
    high = v.astype(BF16)
    return high, (v - high.astype(F32)).astype(BF16)


def dot_split(a_twice, b):
    high, low = split(a_twice)
    size = a_twice.shape[0]
    lane = lax.broadcasted_iota(jnp.int32, a_twice.shape, 1)
    mixed = jnp.where(lane < size, high.astype(F32), low.astype(F32)).astype(BF16)
    b_high, b_low = split(b)
    return dot(jnp.concatenate([mixed, mixed], axis=1), jnp.concatenate([b_high, b_high, b_low, b_low], axis=0))


def shifted(v):
    width = v.shape[1]
    return jnp.concatenate([pltpu.roll(v, 1, 1), v, pltpu.roll(v, width - 1, 1)], axis=0)


def gathered(parts, width):
    third = parts.shape[0] // 3
    sums = []
    for at in range(0, parts.shape[1], width):
        part = parts[:, at : at + width]
        left, right = pltpu.roll(part[:third], 1, 1), pltpu.roll(part[2 * third :], width - 1, 1)
        sums.append(part[third : 2 * third] + left + right)
    return jnp.concatenate(sums, axis=1)


def tap_rows(load, padded):
    lines = []
    for dx in range(3):
        parts = [load(3 * dy + dx) for dy in range(3)]
        filler = jnp.zeros((parts[0].shape[0], padded - 3 * parts[0].shape[1]), F32)
        lines.append(jnp.concatenate([*parts, filler], axis=1))
    return jnp.concatenate(lines, axis=0)


def kernel(sizes, *refs):
    n_member, n_tile, members, fields, rows, width, channels, depth, kept, lanes, halves, chunks = sizes
    edge_lanes, own_lanes = lanes
    middle = depth - 2
    sources, out_ref, refs = refs[:9], refs[9], refs[10:]
    fetched, refs = refs[:9], refs[9:]
    (
        state_ref, spread_ref, first_ref, middle_ref, last_ref, observed_ref, variance_ref, rows_ref, class_ref,
    ) = fetched
    taps_first, taps_own, taps_edge, refs = refs[0], refs[1], refs[2], refs[3:]
    taps_middle, refs = refs[:middle], refs[middle:]
    (
        taps_last, mixed, onehot, halo_out, halo_in, outbox, inbox, back_out, back_in, fetch_sem,
        halo_send, halo_recv, fore_send, fore_recv, back_send, back_recv,
    ) = refs
    fetches = [
        pltpu.make_async_copy(source, target, fetch_sem.at[n])
        for n, (source, target) in enumerate(zip(sources, fetched))
    ]
    fetches[0].start()
    me = lax.axis_index("member")
    tile = lax.axis_index("tile")
    block = fields * rows
    ensemble = n_member * members
    span = fields * width

    def wrapped(index, count):
        index = jnp.where(index >= count, index - count, index)
        return jnp.where(index < 0, index + count, index)

    def tile_at(shift):
        return wrapped(tile + shift, n_tile) if shift else tile

    def member_at(shift):
        return wrapped(me + shift, n_member) if shift else me

    barrier = pltpu.get_barrier_semaphore()
    peers = [(i, d) for d in (1, -1, 0) for i in range(n_member) if (i, d) != (0, 0)]
    for i, d in peers:
        pl.semaphore_signal(barrier, inc=1, device_id=(member_at(i), tile_at(d)), device_id_type=MESH)

    for fetch in fetches[1:]:
        fetch.start()
    fetches[0].wait()
    for m in range(members):
        whole = state_ref[m].astype(F32)
        each = [whole[f * rows : (f + 1) * rows] for f in range(fields)]
        halo_out[0, m] = jnp.concatenate([v[rows - kept :] for v in each], axis=0).astype(BF16)
        halo_out[1, m] = jnp.concatenate([v[:kept] for v in each], axis=0).astype(BF16)
    pl.semaphore_wait(barrier, len(peers))
    halo_copies = []
    for side, d in ((0, 1), (1, -1)):
        copy = pltpu.make_async_remote_copy(
            src_ref=halo_out.at[side],
            dst_ref=halo_in.at[side],
            send_sem=halo_send.at[side],
            recv_sem=halo_recv.at[side],
            device_id=(me, tile_at(d)),
            device_id_type=MESH,
        )
        copy.start()
        halo_copies.append(copy)

    with jax.named_scope("taps"):
        for fetch in fetches[1:]:
            fetch.wait()
        first_taps = jnp.concatenate([first_ref[n].astype(F32) for n in range(9)], axis=0).astype(BF16)
        wide = lax.dot_general(
            first_taps, spread_ref[...], (((0,), (0,)), ((), ())), preferred_element_type=F32
        ).astype(BF16)
        count = taps_first.shape[1]
        for r in range(2 * depth):
            taps_first[r * channels : (r + 1) * channels, :] = wide[:, r * edge_lanes : r * edge_lanes + count]
        begin = 2 * depth * edge_lanes
        count = taps_own.shape[1]
        for r in range(rows - 2):
            taps_own[r * channels : (r + 1) * channels, :] = wide[:, begin + r * own_lanes : begin + r * own_lanes + count]
        for number in range(middle):
            chunk = max(chunks[number], depth)
            base = tap_rows(lambda n: middle_ref[9 * number + n].astype(F32), -(-(chunk + 2) * channels // 128) * 128)
            spread_middle(taps_middle[number], base, chunks[number], channels)
            if number == 0:
                spread_middle(taps_edge, base, depth, channels)
        inner = (rows + 2) * channels
        padded = -(-inner // 128) * 128
        base = tap_rows(lambda n: last_ref[n].astype(F32), padded)
        base = jnp.broadcast_to(base[:, None, :], (base.shape[0], rows, padded)).reshape(-1, padded)
        row_of = lax.rem(lax.broadcasted_iota(jnp.int32, base.shape, 0), rows)
        total = jnp.where(row_of == 0, base, 0.0)
        for r in range(1, rows):
            total = total + jnp.where(row_of == r, pltpu.roll(base, r * channels, 1), 0.0)
        taps_last[...] = total.astype(BF16)[:, :inner]

    share = members // halves
    group = 2 if share % 2 == 0 else 1
    groups = [range(start, start + group) for start in range(0, members, group)]

    own_first = []
    for ids in groups:
        stacked = [shifted(state_ref[m].astype(F32)) for m in ids]
        own_first.append(silu(dot(taps_own[...], jnp.concatenate(stacked, axis=1).astype(BF16))).astype(BF16))
    own_second = [middle_layer(taps_middle[0][...], v, chunks[0], channels, width) for v in own_first]

    for copy in halo_copies:
        copy.wait_recv()

    fore_copies = {}
    for half in range(halves):
        edge_first = []
        for ids in groups:
            stacked = [
                shifted(jnp.concatenate([halo_in[0, m], state_ref[m], halo_in[1, m]], axis=0).astype(F32))
                for m in ids
            ]
            edge_first.append(silu(dot(taps_first[...], jnp.concatenate(stacked, axis=1).astype(BF16))).astype(BF16))
        hidden = []
        cut = depth * channels
        for edge, own, second in zip(edge_first, own_first, own_second):
            above = jnp.concatenate([edge[:cut], own[: 2 * channels]], axis=0)
            below = jnp.concatenate([own[(rows - 4) * channels :], edge[cut:]], axis=0)
            above = middle_layer(taps_edge[...], above, depth, channels, width)
            below = middle_layer(taps_edge[...], below, depth, channels, width)
            hidden.append(jnp.concatenate([above, second, below], axis=0))
        for number in range(1, middle):
            hidden = [middle_layer(taps_middle[number][...], v, chunks[number], channels, width) for v in hidden]
        for ids, before in zip(groups, hidden):
            change = gathered(dot(taps_last[...], before), width)
            for g, m in enumerate(ids):
                mixed[m * block : (m + 1) * block, :] = (
                    state_ref[m].astype(F32) + change[:, g * width : (g + 1) * width]
                )

        for r in range(rows):
            outbox[half, r] = jnp.concatenate(
                [mixed[pl.ds(half * share * block + f * rows + r, share, stride=block), :] for f in range(fields)],
                axis=0,
            ).astype(BF16)

        for s in (0, 2, 1):
            for i in range(n_member):
                if s == 1 and i == 0:
                    continue
                target = member_at(i)
                copy = pltpu.make_async_remote_copy(
                    src_ref=outbox.at[half, target],
                    dst_ref=inbox.at[s, half, me],
                    send_sem=fore_send.at[s, half, i],
                    recv_sem=fore_recv.at[s, half, i],
                    device_id=(target, tile_at(1 - s)),
                    device_id_type=MESH,
                )
                copy.start()
                fore_copies[s, half, i] = copy
        inbox[1, half, me] = outbox[half, me]

    read = rows_ref[...]
    spot = lax.broadcasted_iota(jnp.int32, (span, read.shape[1]), 0)
    for s in range(3):
        onehot[s] = jnp.where(spot == read - s * span, 1.0, 0.0).astype(BF16)
    obs_weight = jnp.exp(-0.25 * class_ref[...].astype(F32)) / variance_ref[...]
    eye_row = lax.broadcasted_iota(jnp.int32, (ensemble, 2 * ensemble), 0)
    eye_col = lax.broadcasted_iota(jnp.int32, (ensemble, 2 * ensemble), 1)
    identity = jnp.where((eye_row == eye_col) | (eye_row + ensemble == eye_col), 1.0, 0.0).astype(F32)

    def neighbour(s):
        blocks = [inbox[s, half, k].astype(F32) for k in range(n_member) for half in range(halves)]
        columns = [
            jnp.concatenate([b[f * share : (f + 1) * share] for b in blocks], axis=0) for f in range(fields)
        ]
        return jnp.concatenate(columns, axis=1)

    obs_ens = None
    back = None
    for s in (1, 0, 2):
        for half in range(halves):
            for i in range(n_member):
                if (s, half, i) in fore_copies:
                    fore_copies[s, half, i].wait_recv()
        values = neighbour(s)
        if s == 1:
            back = values
        part = dot(values.astype(BF16), onehot[s])
        obs_ens = part if obs_ens is None else obs_ens + part

    obs_mean = jnp.sum(obs_ens, axis=0, keepdims=True) / ensemble
    obs_anom = obs_ens - obs_mean
    anom_high, anom_low = split(obs_anom)
    heavy_high, heavy_low = split(obs_weight * obs_anom)
    gram = (ensemble - 1.0) * identity + lax.dot_general(
        jnp.concatenate([anom_high, anom_low, anom_high], axis=1),
        jnp.concatenate([jnp.concatenate([heavy_high, heavy_high, heavy_low], axis=1)] * 2, axis=0),
        (((1,), (1,)), ((), ())),
        preferred_element_type=F32,
    )
    residual = jnp.sum(obs_anom * (obs_weight * (observed_ref[...] - obs_mean)), axis=1, keepdims=True)
    norm_scale = jnp.sqrt(0.5 * jnp.sum(gram * gram, keepdims=True))
    iterate_y = gram / norm_scale
    iterate_z = 1.5 * identity - 0.5 * iterate_y
    iterate_y = dot_split(iterate_y, iterate_z)
    for sweep in range(1, NS_ITERS):
        factor = 1.5 * identity - 0.5 * dot_split(iterate_z, iterate_y)
        if sweep + 1 < NS_ITERS:
            iterate_y = dot_split(iterate_y, factor)
        iterate_z = dot_split(factor, iterate_z)
    root_inv = iterate_z / jnp.sqrt(norm_scale)
    back_mean = jnp.sum(back, axis=0, keepdims=True) / ensemble
    back_anom = back - back_mean
    both = dot_split(root_inv, jnp.concatenate([back_anom, jnp.broadcast_to(residual, (ensemble, 128))], axis=1))
    moved, pull = both[:, :span], both[:, span : span + 1]
    shift = back_mean + jnp.sum(pull * moved, axis=0, keepdims=True)
    analysed = shift + (ensemble - 1.0) ** 0.5 * moved

    for k in range(n_member):
        rows_k = analysed[k * members : (k + 1) * members]
        back_out[k] = jnp.concatenate(
            [rows_k[:, f * width : (f + 1) * width] for f in range(fields)], axis=0
        ).astype(BF16)
    back_copies = []
    for i in range(1, n_member):
        target = member_at(i)
        copy = pltpu.make_async_remote_copy(
            src_ref=back_out.at[target],
            dst_ref=back_in.at[me],
            send_sem=back_send.at[i],
            recv_sem=back_recv.at[i],
            device_id=(target, tile),
            device_id_type=MESH,
        )
        copy.start()
        back_copies.append(copy)
    back_in[me] = back_out[me]
    for copy in halo_copies:
        copy.wait_send()
    for copy in fore_copies.values():
        copy.wait_send()
    for copy in back_copies:
        copy.wait_recv()
    pack = fields * members
    for r in range(rows):
        mixed[r * pack : (r + 1) * pack, :] = back_in[r].astype(F32)
    for m in range(members):
        out_ref[m] = jnp.concatenate(
            [mixed[pl.ds(f * members + m, rows, stride=pack), :] for f in range(fields)], axis=0
        ).astype(BF16)
    for copy in back_copies:
        copy.wait_send()


def local(state, first_weight, middle_weight, last_weight, observations, obs_variance, observation_rows, loc_class):
    members, fields, rows, width = state.shape
    channels = first_weight.shape[0]
    middle = middle_weight.shape[0]
    depth = middle + 2
    n_member = lax.axis_size("member")
    n_tile = lax.axis_size("tile")
    assert rows == n_member and n_tile >= 3
    kept = depth
    while fields * kept % 16:
        kept += 1
    assert kept <= rows and rows > 4
    block = fields * rows
    first_rows = rows + 2 * (depth - 1)
    obs = observations.shape[2]
    span = fields * width
    whole_lines = [(f, depth - kept + q) for f in range(fields) for q in range(kept)]
    own_lines = [(f, depth + r) for f in range(fields) for r in range(rows)]
    whole_lines += own_lines + [(f, depth + rows + q) for f in range(fields) for q in range(kept)]
    own_rows = range(depth, depth + rows - 2)
    edge_rows = [r for r in range(first_rows) if r not in own_rows]
    lanes = tuple(-(-3 * len(lines) // 128) * 128 for lines in (whole_lines, own_lines))
    spread = jnp.asarray(
        np.concatenate(
            [
                first_selector(fields, whole_lines, edge_rows, lanes[0]),
                first_selector(fields, own_lines, own_rows, lanes[1]),
            ],
            axis=1,
        ),
        BF16,
    )
    operands = (
        state.reshape(members, block, width),
        spread,
        jnp.transpose(first_weight, (2, 3, 1, 0)).reshape(9, fields, channels),
        jnp.transpose(middle_weight, (0, 3, 4, 1, 2)).reshape(9 * middle, channels, channels),
        jnp.transpose(last_weight, (2, 3, 0, 1)).reshape(9, fields, channels),
        observations[0],
        obs_variance[0],
        observation_rows[0],
        loc_class[0],
    )
    halves = 1
    chunks = []
    for n in range(middle):
        out_rows = rows + 2 * (depth - 2 - n) if n else rows - 4
        most = max(1, 256 // channels - 2)
        chunks.append(max(c for c in range(1, out_rows + 1) if out_rows % c == 0 and c <= most))
    sizes = (n_member, n_tile, members, fields, rows, width, channels, depth, kept, lanes, halves, chunks)
    vmem = pl.BlockSpec(memory_space=pltpu.VMEM)
    packet = (fields * members, width)
    out = pl.pallas_call(
        functools.partial(kernel, sizes),
        out_shape=pltpu.VMEM((members, block, width), BF16),
        in_specs=[pl.BlockSpec(memory_space=pltpu.HBM)] * len(operands),
        out_specs=vmem,
        scratch_shapes=[
            *[pltpu.VMEM(v.shape, v.dtype) for v in operands],
            pltpu.VMEM((2 * depth * channels, 3 * len(whole_lines)), BF16),
            pltpu.VMEM(((rows - 2) * channels, 3 * len(own_lines)), BF16),
            pltpu.VMEM((3 * depth * channels, (depth + 2) * channels), BF16),
            *[
                pltpu.VMEM((3 * chunks[n] * channels, (chunks[n] + 2) * channels), BF16)
                for n in range(middle)
            ],
            pltpu.VMEM((3 * block, (rows + 2) * channels), BF16),
            pltpu.VMEM((members * block, width), F32),
            pltpu.VMEM((3, span, obs), BF16),
            pltpu.VMEM((2, members, fields * kept, width), BF16),
            pltpu.VMEM((2, members, fields * kept, width), BF16),
            pltpu.VMEM((halves, n_member, fields * members // halves, width), BF16),
            pltpu.VMEM((3, halves, n_member, fields * members // halves, width), BF16),
            pltpu.VMEM((n_member, *packet), BF16),
            pltpu.VMEM((n_member, *packet), BF16),
            pltpu.SemaphoreType.DMA((len(operands),)),
            pltpu.SemaphoreType.DMA((2,)),
            pltpu.SemaphoreType.DMA((2,)),
            pltpu.SemaphoreType.DMA((3, halves, n_member)),
            pltpu.SemaphoreType.DMA((3, halves, n_member)),
            pltpu.SemaphoreType.DMA((n_member,)),
            pltpu.SemaphoreType.DMA((n_member,)),
        ],
        compiler_params=pltpu.CompilerParams(
            collective_id=0, has_side_effects=True, vmem_limit_bytes=60 * 1024 * 1024
        ),
    )(*operands)
    return out.reshape(members, fields, rows, width)


def solution(mesh):
    return jax.shard_map(
        local,
        mesh=mesh,
        in_specs=(
            P("member", None, "tile", None),
            P(),
            P(),
            P(),
            P("tile", "member", None),
            P("tile", "member", None),
            P("tile", "member", None),
            P("tile", "member", None),
        ),
        out_specs=P("member", None, "tile", None),
        check_vma=False,
    )
```

```python
import functools

import jax
import jax.numpy as jnp
import numpy as np
from jax import lax
from jax.experimental import pallas as pl
from jax.experimental.pallas import tpu as pltpu
from jax.sharding import PartitionSpec as P

NS_ITERS = 4
MESH = pl.DeviceIdType.MESH
F32 = jnp.float32
BF16 = jnp.bfloat16


def silu(v):
    half = 0.5 * v
    return half + half * jnp.tanh(half)


def first_selector(fields, where, out_rows, lanes):
    spread = np.zeros((3, 3, fields, len(out_rows), lanes), np.float32)
    for dx in range(3):
        for k, (f, row) in enumerate(where):
            for n, r in enumerate(out_rows):
                if 0 <= row - r <= 2:
                    spread[row - r, dx, f, n, dx * len(where) + k] = 1
    return spread.reshape(9 * fields, len(out_rows) * lanes)


def middle_layer(taps, hidden, chunk, channels, width):
    count = hidden.shape[0] // channels - 2
    parts = [
        silu(gathered(dot(taps, hidden[r * channels : (r + chunk + 2) * channels]), width)).astype(BF16)
        for r in range(0, count, chunk)
    ]
    return jnp.concatenate(parts, axis=0)


def spread_middle(taps, base, chunk, channels):
    inner = (chunk + 2) * channels
    for r in range(chunk):
        moved = (pltpu.roll(base, r * channels, 1) if r else base).astype(BF16)
        for dx in range(3):
            at = (dx * chunk + r) * channels
            taps[at : at + channels, :] = moved[dx * channels : (dx + 1) * channels, :inner]


def dot(a, b):
    return jnp.dot(a, b, preferred_element_type=F32)


def split(v):
    high = v.astype(BF16)
    return high, (v - high.astype(F32)).astype(BF16)


def dot_split(a_twice, b):
    high, low = split(a_twice)
    size = a_twice.shape[0]
    lane = lax.broadcasted_iota(jnp.int32, a_twice.shape, 1)
    mixed = jnp.where(lane < size, high.astype(F32), low.astype(F32)).astype(BF16)
    b_high, b_low = split(b)
    return dot(jnp.concatenate([mixed, mixed], axis=1), jnp.concatenate([b_high, b_high, b_low, b_low], axis=0))


def shifted(v):
    width = v.shape[1]
    return jnp.concatenate([pltpu.roll(v, 1, 1), v, pltpu.roll(v, width - 1, 1)], axis=0)


def gathered(parts, width):
    third = parts.shape[0] // 3
    sums = []
    for at in range(0, parts.shape[1], width):
        part = parts[:, at : at + width]
        left, right = pltpu.roll(part[:third], 1, 1), pltpu.roll(part[2 * third :], width - 1, 1)
        sums.append(part[third : 2 * third] + left + right)
    return jnp.concatenate(sums, axis=1)


def tap_rows(load, padded):
    lines = []
    for dx in range(3):
        parts = [load(3 * dy + dx) for dy in range(3)]
        filler = jnp.zeros((parts[0].shape[0], padded - 3 * parts[0].shape[1]), F32)
        lines.append(jnp.concatenate([*parts, filler], axis=1))
    return jnp.concatenate(lines, axis=0)


def kernel(sizes, *refs):
    n_member, n_tile, members, fields, rows, width, channels, depth, kept, lanes, halves, chunks = sizes
    edge_lanes, own_lanes = lanes
    middle = depth - 2
    sources, out_ref, refs = refs[:9], refs[9], refs[10:]
    fetched, refs = refs[:9], refs[9:]
    (
        state_ref, spread_ref, first_ref, middle_ref, last_ref, observed_ref, variance_ref, rows_ref, class_ref,
    ) = fetched
    taps_first, taps_own, taps_edge, refs = refs[0], refs[1], refs[2], refs[3:]
    taps_middle, refs = refs[:middle], refs[middle:]
    (
        taps_last, mixed, onehot, halo_out, halo_in, outbox, inbox, back_out, back_in, fetch_sem,
        halo_send, halo_recv, fore_send, fore_recv, back_send, back_recv,
    ) = refs
    fetches = [
        pltpu.make_async_copy(source, target, fetch_sem.at[n])
        for n, (source, target) in enumerate(zip(sources, fetched))
    ]
    fetches[0].start()
    me = lax.axis_index("member")
    tile = lax.axis_index("tile")
    block = fields * rows
    ensemble = n_member * members
    span = fields * width

    def wrapped(index, count):
        index = jnp.where(index >= count, index - count, index)
        return jnp.where(index < 0, index + count, index)

    def tile_at(shift):
        return wrapped(tile + shift, n_tile) if shift else tile

    def member_at(shift):
        return wrapped(me + shift, n_member) if shift else me

    barrier = pltpu.get_barrier_semaphore()
    peers = [(i, d) for d in (1, -1, 0) for i in range(n_member) if (i, d) != (0, 0)]
    for i, d in peers:
        pl.semaphore_signal(barrier, inc=1, device_id=(member_at(i), tile_at(d)), device_id_type=MESH)

    for fetch in fetches[1:]:
        fetch.start()
    fetches[0].wait()
    for m in range(members):
        whole = state_ref[m].astype(F32)
        each = [whole[f * rows : (f + 1) * rows] for f in range(fields)]
        halo_out[0, m] = jnp.concatenate([v[rows - kept :] for v in each], axis=0).astype(BF16)
        halo_out[1, m] = jnp.concatenate([v[:kept] for v in each], axis=0).astype(BF16)
    pl.semaphore_wait(barrier, len(peers))
    halo_copies = []
    for side, d in ((0, 1), (1, -1)):
        copy = pltpu.make_async_remote_copy(
            src_ref=halo_out.at[side],
            dst_ref=halo_in.at[side],
            send_sem=halo_send.at[side],
            recv_sem=halo_recv.at[side],
            device_id=(me, tile_at(d)),
            device_id_type=MESH,
        )
        copy.start()
        halo_copies.append(copy)

    with jax.named_scope("taps"):
        for fetch in fetches[1:]:
            fetch.wait()
        first_taps = jnp.concatenate([first_ref[n].astype(F32) for n in range(9)], axis=0).astype(BF16)
        wide = lax.dot_general(
            first_taps, spread_ref[...], (((0,), (0,)), ((), ())), preferred_element_type=F32
        ).astype(BF16)
        count = taps_first.shape[1]
        for r in range(2 * depth):
            taps_first[r * channels : (r + 1) * channels, :] = wide[:, r * edge_lanes : r * edge_lanes + count]
        begin = 2 * depth * edge_lanes
        count = taps_own.shape[1]
        for r in range(rows - 2):
            taps_own[r * channels : (r + 1) * channels, :] = wide[:, begin + r * own_lanes : begin + r * own_lanes + count]
        for number in range(middle):
            chunk = max(chunks[number], depth)
            base = tap_rows(lambda n: middle_ref[9 * number + n].astype(F32), -(-(chunk + 2) * channels // 128) * 128)
            spread_middle(taps_middle[number], base, chunks[number], channels)
            if number == 0:
                spread_middle(taps_edge, base, depth, channels)
        inner = (rows + 2) * channels
        padded = -(-inner // 128) * 128
        base = tap_rows(lambda n: last_ref[n].astype(F32), padded)
        base = jnp.broadcast_to(base[:, None, :], (base.shape[0], rows, padded)).reshape(-1, padded)
        row_of = lax.rem(lax.broadcasted_iota(jnp.int32, base.shape, 0), rows)
        total = jnp.where(row_of == 0, base, 0.0)
        for r in range(1, rows):
            total = total + jnp.where(row_of == r, pltpu.roll(base, r * channels, 1), 0.0)
        taps_last[...] = total.astype(BF16)[:, :inner]

    share = members // halves
    group = 2 if share % 2 == 0 else 1
    groups = [range(start, start + group) for start in range(0, members, group)]

    own_first = []
    for ids in groups:
        stacked = [shifted(state_ref[m].astype(F32)) for m in ids]
        own_first.append(silu(dot(taps_own[...], jnp.concatenate(stacked, axis=1).astype(BF16))).astype(BF16))
    own_second = [middle_layer(taps_middle[0][...], v, chunks[0], channels, width) for v in own_first]

    for copy in halo_copies:
        copy.wait_recv()

    for half in range(halves):
        edge_first = []
        for ids in groups:
            stacked = [
                shifted(jnp.concatenate([halo_in[0, m], state_ref[m], halo_in[1, m]], axis=0).astype(F32))
                for m in ids
            ]
            edge_first.append(silu(dot(taps_first[...], jnp.concatenate(stacked, axis=1).astype(BF16))).astype(BF16))
        hidden = []
        cut = depth * channels
        for edge, own, second in zip(edge_first, own_first, own_second):
            above = jnp.concatenate([edge[:cut], own[: 2 * channels]], axis=0)
            below = jnp.concatenate([own[(rows - 4) * channels :], edge[cut:]], axis=0)
            above = middle_layer(taps_edge[...], above, depth, channels, width)
            below = middle_layer(taps_edge[...], below, depth, channels, width)
            hidden.append(jnp.concatenate([above, second, below], axis=0))
        for number in range(1, middle):
            hidden = [middle_layer(taps_middle[number][...], v, chunks[number], channels, width) for v in hidden]
        for ids, before in zip(groups, hidden):
            change = gathered(dot(taps_last[...], before), width)
            for g, m in enumerate(ids):
                mixed[m * block : (m + 1) * block, :] = (
                    state_ref[m].astype(F32) + change[:, g * width : (g + 1) * width]
                )

        for r in range(rows):
            outbox[half, r] = jnp.concatenate(
                [mixed[pl.ds(half * share * block + f * rows + r, share, stride=block), :] for f in range(fields)],
                axis=0,
            ).astype(BF16)

        for s in (0, 2, 1):
            for i in range(n_member):
                if s == 1 and i == 0:
                    continue
                target = member_at(i)
                copy = pltpu.make_async_remote_copy(
                    src_ref=outbox.at[half, target],
                    dst_ref=inbox.at[s, half, me],
                    send_sem=fore_send.at[s, half],
                    recv_sem=fore_recv.at[s, half],
                    device_id=(target, tile_at(1 - s)),
                    device_id_type=MESH,
                )
                copy.start()
        inbox[1, half, me] = outbox[half, me]

    read = rows_ref[...]
    spot = lax.broadcasted_iota(jnp.int32, (span, read.shape[1]), 0)
    for s in range(3):
        onehot[s] = jnp.where(spot == read - s * span, 1.0, 0.0).astype(BF16)
    obs_weight = jnp.exp(-0.25 * class_ref[...].astype(F32)) / variance_ref[...]
    obs_root = jnp.sqrt(obs_weight)
    eye_row = lax.broadcasted_iota(jnp.int32, (ensemble, 2 * ensemble), 0)
    eye_col = lax.broadcasted_iota(jnp.int32, (ensemble, 2 * ensemble), 1)
    identity = jnp.where((eye_row == eye_col) | (eye_row + ensemble == eye_col), 1.0, 0.0).astype(F32)

    def neighbour(s):
        blocks = [inbox[s, half, k].astype(F32) for k in range(n_member) for half in range(halves)]
        columns = [
            jnp.concatenate([b[f * share : (f + 1) * share] for b in blocks], axis=0) for f in range(fields)
        ]
        return jnp.concatenate(columns, axis=1)

    def arriving(s):
        return n_member - 1 if s == 1 else n_member

    obs_ens = None
    back = None
    for s in (1, 0, 2):
        for half in range(halves):
            packets = inbox.at[s, half, pl.ds(0, arriving(s))]
            pltpu.make_async_copy(packets, packets, fore_recv.at[s, half]).wait()
        values = neighbour(s)
        if s == 1:
            back = values
        part = dot(values.astype(BF16), onehot[s])
        obs_ens = part if obs_ens is None else obs_ens + part

    obs_mean = jnp.sum(obs_ens, axis=0, keepdims=True) / ensemble
    obs_anom = obs_ens - obs_mean
    parts = jnp.concatenate(split(obs_root * obs_anom), axis=0)
    quadrants = lax.dot_general(parts, parts, (((1,), (1,)), ((), ())), preferred_element_type=F32)
    beside = quadrants[:ensemble] + quadrants[ensemble:]
    gram = (ensemble - 1.0) * identity + (beside + pltpu.roll(beside, ensemble, 1))
    residual = jnp.sum(obs_anom * (obs_weight * (observed_ref[...] - obs_mean)), axis=1, keepdims=True)
    norm_scale = jnp.sqrt(0.5 * jnp.sum(gram * gram, keepdims=True))
    iterate_y = gram / norm_scale
    iterate_z = 1.5 * identity - 0.5 * iterate_y
    iterate_y = dot_split(iterate_y, iterate_z)
    for sweep in range(1, NS_ITERS):
        factor = 1.5 * identity - 0.5 * dot_split(iterate_z, iterate_y)
        if sweep + 1 < NS_ITERS:
            iterate_y = dot_split(iterate_y, factor)
        iterate_z = dot_split(factor, iterate_z)
    root_inv = iterate_z / jnp.sqrt(norm_scale)
    back_mean = jnp.sum(back, axis=0, keepdims=True) / ensemble
    back_anom = back - back_mean
    both = dot_split(root_inv, jnp.concatenate([back_anom, jnp.broadcast_to(residual, (ensemble, 128))], axis=1))
    moved, pull = both[:, :span], both[:, span : span + 1]
    shift = back_mean + jnp.sum(pull * moved, axis=0, keepdims=True)
    analysed = shift + (ensemble - 1.0) ** 0.5 * moved

    for k in range(n_member):
        rows_k = analysed[k * members : (k + 1) * members]
        back_out[k] = jnp.concatenate(
            [rows_k[:, f * width : (f + 1) * width] for f in range(fields)], axis=0
        ).astype(BF16)
    for i in range(1, n_member):
        target = member_at(i)
        copy = pltpu.make_async_remote_copy(
            src_ref=back_out.at[target],
            dst_ref=back_in.at[me],
            send_sem=back_send,
            recv_sem=back_recv,
            device_id=(target, tile),
            device_id_type=MESH,
        )
        copy.start()
    back_in[me] = back_out[me]
    for copy in halo_copies:
        copy.wait_send()
    for s in range(3):
        for half in range(halves):
            packets = outbox.at[half, pl.ds(0, arriving(s))]
            pltpu.make_async_copy(packets, packets, fore_send.at[s, half]).wait()
    packets = back_in.at[pl.ds(0, n_member - 1)]
    pltpu.make_async_copy(packets, packets, back_recv).wait()
    pack = fields * members
    for r in range(rows):
        mixed[r * pack : (r + 1) * pack, :] = back_in[r].astype(F32)
    for m in range(members):
        out_ref[m] = jnp.concatenate(
            [mixed[pl.ds(f * members + m, rows, stride=pack), :] for f in range(fields)], axis=0
        ).astype(BF16)
    packets = back_out.at[pl.ds(0, n_member - 1)]
    pltpu.make_async_copy(packets, packets, back_send).wait()


def local(state, first_weight, middle_weight, last_weight, observations, obs_variance, observation_rows, loc_class):
    members, fields, rows, width = state.shape
    channels = first_weight.shape[0]
    middle = middle_weight.shape[0]
    depth = middle + 2
    n_member = lax.axis_size("member")
    n_tile = lax.axis_size("tile")
    assert rows == n_member and n_tile >= 3
    kept = depth
    while fields * kept % 16:
        kept += 1
    assert kept <= rows and rows > 4
    block = fields * rows
    first_rows = rows + 2 * (depth - 1)
    obs = observations.shape[2]
    span = fields * width
    whole_lines = [(f, depth - kept + q) for f in range(fields) for q in range(kept)]
    own_lines = [(f, depth + r) for f in range(fields) for r in range(rows)]
    whole_lines += own_lines + [(f, depth + rows + q) for f in range(fields) for q in range(kept)]
    own_rows = range(depth, depth + rows - 2)
    edge_rows = [r for r in range(first_rows) if r not in own_rows]
    lanes = tuple(-(-3 * len(lines) // 128) * 128 for lines in (whole_lines, own_lines))
    spread = jnp.asarray(
        np.concatenate(
            [
                first_selector(fields, whole_lines, edge_rows, lanes[0]),
                first_selector(fields, own_lines, own_rows, lanes[1]),
            ],
            axis=1,
        ),
        BF16,
    )
    operands = (
        state.reshape(members, block, width),
        spread,
        jnp.transpose(first_weight, (2, 3, 1, 0)).reshape(9, fields, channels),
        jnp.transpose(middle_weight, (0, 3, 4, 1, 2)).reshape(9 * middle, channels, channels),
        jnp.transpose(last_weight, (2, 3, 0, 1)).reshape(9, fields, channels),
        observations[0],
        obs_variance[0],
        observation_rows[0],
        loc_class[0],
    )
    halves = 1
    chunks = []
    for n in range(middle):
        out_rows = rows + 2 * (depth - 2 - n) if n else rows - 4
        most = max(1, 256 // channels - 2)
        chunks.append(max(c for c in range(1, out_rows + 1) if out_rows % c == 0 and c <= most))
    sizes = (n_member, n_tile, members, fields, rows, width, channels, depth, kept, lanes, halves, chunks)
    vmem = pl.BlockSpec(memory_space=pltpu.VMEM)
    packet = (fields * members, width)
    out = pl.pallas_call(
        functools.partial(kernel, sizes),
        out_shape=pltpu.VMEM((members, block, width), BF16),
        in_specs=[pl.BlockSpec(memory_space=pltpu.HBM)] * len(operands),
        out_specs=vmem,
        scratch_shapes=[
            *[pltpu.VMEM(v.shape, v.dtype) for v in operands],
            pltpu.VMEM((2 * depth * channels, 3 * len(whole_lines)), BF16),
            pltpu.VMEM(((rows - 2) * channels, 3 * len(own_lines)), BF16),
            pltpu.VMEM((3 * depth * channels, (depth + 2) * channels), BF16),
            *[
                pltpu.VMEM((3 * chunks[n] * channels, (chunks[n] + 2) * channels), BF16)
                for n in range(middle)
            ],
            pltpu.VMEM((3 * block, (rows + 2) * channels), BF16),
            pltpu.VMEM((members * block, width), F32),
            pltpu.VMEM((3, span, obs), BF16),
            pltpu.VMEM((2, members, fields * kept, width), BF16),
            pltpu.VMEM((2, members, fields * kept, width), BF16),
            pltpu.VMEM((halves, n_member, fields * members // halves, width), BF16),
            pltpu.VMEM((3, halves, n_member, fields * members // halves, width), BF16),
            pltpu.VMEM((n_member, *packet), BF16),
            pltpu.VMEM((n_member, *packet), BF16),
            pltpu.SemaphoreType.DMA((len(operands),)),
            pltpu.SemaphoreType.DMA((2,)),
            pltpu.SemaphoreType.DMA((2,)),
            pltpu.SemaphoreType.DMA((3, halves)),
            pltpu.SemaphoreType.DMA((3, halves)),
            pltpu.SemaphoreType.DMA,
            pltpu.SemaphoreType.DMA,
        ],
        compiler_params=pltpu.CompilerParams(
            collective_id=0, has_side_effects=True, vmem_limit_bytes=60 * 1024 * 1024
        ),
    )(*operands)
    return out.reshape(members, fields, rows, width)


def solution(mesh):
    return jax.shard_map(
        local,
        mesh=mesh,
        in_specs=(
            P("member", None, "tile", None),
            P(),
            P(),
            P(),
            P("tile", "member", None),
            P("tile", "member", None),
            P("tile", "member", None),
            P("tile", "member", None),
        ),
        out_specs=P("member", None, "tile", None),
        check_vma=False,
    )
```

```python
import functools

import jax
import jax.numpy as jnp
import numpy as np
from jax import lax
from jax.experimental import pallas as pl
from jax.experimental.pallas import tpu as pltpu
from jax.sharding import PartitionSpec as P

NS_ITERS = 4
MESH = pl.DeviceIdType.MESH
F32 = jnp.float32
BF16 = jnp.bfloat16


def silu(v):
    half = 0.5 * v
    return half + half * jnp.tanh(half)


def first_selector(fields, where, out_rows, lanes):
    spread = np.zeros((3, 3, fields, len(out_rows), lanes), np.float32)
    for dx in range(3):
        for k, (f, row) in enumerate(where):
            for n, r in enumerate(out_rows):
                if 0 <= row - r <= 2:
                    spread[row - r, dx, f, n, dx * len(where) + k] = 1
    return spread.reshape(9 * fields, len(out_rows) * lanes)


def middle_layer(taps, hidden, chunk, channels, width):
    count = hidden.shape[0] // channels - 2
    parts = [
        silu(gathered(dot(taps, hidden[r * channels : (r + chunk + 2) * channels]), width)).astype(BF16)
        for r in range(0, count, chunk)
    ]
    return jnp.concatenate(parts, axis=0)


def spread_middle(taps, base, chunk, channels):
    inner = (chunk + 2) * channels
    for r in range(chunk):
        moved = (pltpu.roll(base, r * channels, 1) if r else base).astype(BF16)
        for dx in range(3):
            at = (dx * chunk + r) * channels
            taps[at : at + channels, :] = moved[dx * channels : (dx + 1) * channels, :inner]


def dot(a, b):
    return jnp.dot(a, b, preferred_element_type=F32)


def split(v):
    high = v.astype(BF16)
    return high, (v - high.astype(F32)).astype(BF16)


def stacked_parts(b):
    high, low = split(b)
    return jnp.concatenate([high, high, low, low], axis=0)


def dot_split(a_twice, b):
    return dot_stacked(a_twice, stacked_parts(b))


def dot_stacked(a_twice, b_parts):
    high, low = split(a_twice)
    size = a_twice.shape[0]
    lane = lax.broadcasted_iota(jnp.int32, a_twice.shape, 1)
    mixed = jnp.where(lane < size, high.astype(F32), low.astype(F32)).astype(BF16)
    return dot(jnp.concatenate([mixed, mixed], axis=1), b_parts)


def shifted(v):
    width = v.shape[1]
    return jnp.concatenate([pltpu.roll(v, 1, 1), v, pltpu.roll(v, width - 1, 1)], axis=0)


def gathered(parts, width):
    third = parts.shape[0] // 3
    sums = []
    for at in range(0, parts.shape[1], width):
        part = parts[:, at : at + width]
        left, right = pltpu.roll(part[:third], 1, 1), pltpu.roll(part[2 * third :], width - 1, 1)
        sums.append(part[third : 2 * third] + left + right)
    return jnp.concatenate(sums, axis=1)


def tap_rows(load, padded):
    lines = []
    for dx in range(3):
        parts = [load(3 * dy + dx) for dy in range(3)]
        filler = jnp.zeros((parts[0].shape[0], padded - 3 * parts[0].shape[1]), F32)
        lines.append(jnp.concatenate([*parts, filler], axis=1))
    return jnp.concatenate(lines, axis=0)


def kernel(sizes, *refs):
    n_member, n_tile, members, fields, rows, width, channels, depth, kept, lanes, halves, chunks = sizes
    edge_lanes, own_lanes = lanes
    middle = depth - 2
    sources, out_ref, refs = refs[:9], refs[9], refs[10:]
    fetched, refs = refs[:9], refs[9:]
    (
        state_ref, spread_ref, first_ref, middle_ref, last_ref, observed_ref, variance_ref, rows_ref, class_ref,
    ) = fetched
    taps_first, taps_own, taps_edge, refs = refs[0], refs[1], refs[2], refs[3:]
    taps_middle, refs = refs[:middle], refs[middle:]
    (
        taps_last, mixed, onehot, halo_out, halo_in, outbox, inbox, back_out, back_in, fetch_sem,
        halo_send, halo_recv, fore_send, fore_recv, back_send, back_recv,
    ) = refs
    fetches = [
        pltpu.make_async_copy(source, target, fetch_sem.at[n])
        for n, (source, target) in enumerate(zip(sources, fetched))
    ]
    fetches[0].start()
    me = lax.axis_index("member")
    tile = lax.axis_index("tile")
    block = fields * rows
    ensemble = n_member * members
    span = fields * width

    def wrapped(index, count):
        index = jnp.where(index >= count, index - count, index)
        return jnp.where(index < 0, index + count, index)

    def tile_at(shift):
        return wrapped(tile + shift, n_tile) if shift else tile

    def member_at(shift):
        return wrapped(me + shift, n_member) if shift else me

    barrier = pltpu.get_barrier_semaphore()
    peers = [(i, d) for d in (1, -1, 0) for i in range(n_member) if (i, d) != (0, 0)]
    for i, d in peers:
        pl.semaphore_signal(barrier, inc=1, device_id=(member_at(i), tile_at(d)), device_id_type=MESH)

    for fetch in fetches[1:]:
        fetch.start()
    fetches[0].wait()
    for m in range(members):
        whole = state_ref[m].astype(F32)
        each = [whole[f * rows : (f + 1) * rows] for f in range(fields)]
        halo_out[0, m] = jnp.concatenate([v[rows - kept :] for v in each], axis=0).astype(BF16)
        halo_out[1, m] = jnp.concatenate([v[:kept] for v in each], axis=0).astype(BF16)
    pl.semaphore_wait(barrier, len(peers))
    halo_copies = []
    for side, d in ((0, 1), (1, -1)):
        copy = pltpu.make_async_remote_copy(
            src_ref=halo_out.at[side],
            dst_ref=halo_in.at[side],
            send_sem=halo_send.at[side],
            recv_sem=halo_recv.at[side],
            device_id=(me, tile_at(d)),
            device_id_type=MESH,
        )
        copy.start()
        halo_copies.append(copy)

    with jax.named_scope("taps"):
        for fetch in fetches[1:]:
            fetch.wait()
        first_taps = jnp.concatenate([first_ref[n].astype(F32) for n in range(9)], axis=0).astype(BF16)
        wide = lax.dot_general(
            first_taps, spread_ref[...], (((0,), (0,)), ((), ())), preferred_element_type=F32
        ).astype(BF16)
        count = taps_first.shape[1]
        for r in range(2 * depth):
            taps_first[r * channels : (r + 1) * channels, :] = wide[:, r * edge_lanes : r * edge_lanes + count]
        begin = 2 * depth * edge_lanes
        count = taps_own.shape[1]
        for r in range(rows - 2):
            taps_own[r * channels : (r + 1) * channels, :] = wide[:, begin + r * own_lanes : begin + r * own_lanes + count]
        for number in range(middle):
            chunk = max(chunks[number], depth)
            base = tap_rows(lambda n: middle_ref[9 * number + n].astype(F32), -(-(chunk + 2) * channels // 128) * 128)
            spread_middle(taps_middle[number], base, chunks[number], channels)
            if number == 0:
                spread_middle(taps_edge, base, depth, channels)
        inner = (rows + 2) * channels
        padded = -(-inner // 128) * 128
        base = tap_rows(lambda n: last_ref[n].astype(F32), padded)
        base = jnp.broadcast_to(base[:, None, :], (base.shape[0], rows, padded)).reshape(-1, padded)
        row_of = lax.rem(lax.broadcasted_iota(jnp.int32, base.shape, 0), rows)
        total = jnp.where(row_of == 0, base, 0.0)
        for r in range(1, rows):
            total = total + jnp.where(row_of == r, pltpu.roll(base, r * channels, 1), 0.0)
        taps_last[...] = total.astype(BF16)[:, :inner]

    share = members // halves
    group = 2 if share % 2 == 0 else 1
    groups = [range(start, start + group) for start in range(0, members, group)]

    own_first = []
    for ids in groups:
        stacked = [shifted(state_ref[m].astype(F32)) for m in ids]
        own_first.append(silu(dot(taps_own[...], jnp.concatenate(stacked, axis=1).astype(BF16))).astype(BF16))
    own_second = [middle_layer(taps_middle[0][...], v, chunks[0], channels, width) for v in own_first]

    for copy in halo_copies:
        copy.wait_recv()

    for half in range(halves):
        edge_first = []
        for ids in groups:
            stacked = [
                shifted(jnp.concatenate([halo_in[0, m], state_ref[m], halo_in[1, m]], axis=0).astype(F32))
                for m in ids
            ]
            edge_first.append(silu(dot(taps_first[...], jnp.concatenate(stacked, axis=1).astype(BF16))).astype(BF16))
        hidden = []
        cut = depth * channels
        for edge, own, second in zip(edge_first, own_first, own_second):
            above = jnp.concatenate([edge[:cut], own[: 2 * channels]], axis=0)
            below = jnp.concatenate([own[(rows - 4) * channels :], edge[cut:]], axis=0)
            above = middle_layer(taps_edge[...], above, depth, channels, width)
            below = middle_layer(taps_edge[...], below, depth, channels, width)
            hidden.append(jnp.concatenate([above, second, below], axis=0))
        for number in range(1, middle):
            hidden = [middle_layer(taps_middle[number][...], v, chunks[number], channels, width) for v in hidden]
        for ids, before in zip(groups, hidden):
            change = gathered(dot(taps_last[...], before), width)
            for g, m in enumerate(ids):
                mixed[m * block : (m + 1) * block, :] = (
                    state_ref[m].astype(F32) + change[:, g * width : (g + 1) * width]
                )

        for r in range(rows):
            outbox[half, r] = jnp.concatenate(
                [mixed[pl.ds(half * share * block + f * rows + r, share, stride=block), :] for f in range(fields)],
                axis=0,
            ).astype(BF16)

        for s in (0, 2, 1):
            for i in range(n_member):
                if s == 1 and i == 0:
                    continue
                target = member_at(i)
                copy = pltpu.make_async_remote_copy(
                    src_ref=outbox.at[half, target],
                    dst_ref=inbox.at[s, half, me],
                    send_sem=fore_send.at[s, half],
                    recv_sem=fore_recv.at[s, half],
                    device_id=(target, tile_at(1 - s)),
                    device_id_type=MESH,
                )
                copy.start()
        inbox[1, half, me] = outbox[half, me]

    read = rows_ref[...]
    spot = lax.broadcasted_iota(jnp.int32, (span, read.shape[1]), 0)
    for s in range(3):
        onehot[s] = jnp.where(spot == read - s * span, 1.0, 0.0).astype(BF16)
    obs_weight = jnp.exp(-0.25 * class_ref[...].astype(F32)) / variance_ref[...]
    obs_root = jnp.sqrt(obs_weight)
    eye_row = lax.broadcasted_iota(jnp.int32, (ensemble, 2 * ensemble), 0)
    eye_col = lax.broadcasted_iota(jnp.int32, (ensemble, 2 * ensemble), 1)
    identity = jnp.where((eye_row == eye_col) | (eye_row + ensemble == eye_col), 1.0, 0.0).astype(F32)

    def neighbour(s):
        blocks = [inbox[s, half, k].astype(F32) for k in range(n_member) for half in range(halves)]
        columns = [
            jnp.concatenate([b[f * share : (f + 1) * share] for b in blocks], axis=0) for f in range(fields)
        ]
        return jnp.concatenate(columns, axis=1)

    def arriving(s):
        return n_member - 1 if s == 1 else n_member

    obs_ens = None
    for s in (1, 0, 2):
        for half in range(halves):
            packets = inbox.at[s, half, pl.ds(0, arriving(s))]
            pltpu.make_async_copy(packets, packets, fore_recv.at[s, half]).wait()
        values = neighbour(s)
        if s == 1:
            back_mean = jnp.sum(values, axis=0, keepdims=True) / ensemble
            back_anom = stacked_parts(values - back_mean)
        part = dot(values.astype(BF16), onehot[s])
        obs_ens = part if obs_ens is None else obs_ens + part

    obs_mean = jnp.sum(obs_ens, axis=0, keepdims=True) / ensemble
    obs_anom = obs_ens - obs_mean
    parts = jnp.concatenate(split(obs_root * obs_anom), axis=0)
    quadrants = lax.dot_general(parts, parts, (((1,), (1,)), ((), ())), preferred_element_type=F32)
    beside = quadrants[:ensemble] + quadrants[ensemble:]
    gram = (ensemble - 1.0) * identity + (beside + pltpu.roll(beside, ensemble, 1))
    residual = jnp.sum(obs_anom * (obs_weight * (observed_ref[...] - obs_mean)), axis=1, keepdims=True)
    norm_scale = jnp.sqrt(0.5 * jnp.sum(gram * gram, keepdims=True))
    iterate_y = gram / norm_scale
    iterate_z = 1.5 * identity - 0.5 * iterate_y
    iterate_y = dot_split(iterate_y, iterate_z)
    for sweep in range(1, NS_ITERS):
        factor = 1.5 * identity - 0.5 * dot_split(iterate_z, iterate_y)
        if sweep + 1 < NS_ITERS:
            iterate_y = dot_split(iterate_y, factor)
        iterate_z = dot_split(factor, iterate_z)
    root_inv = iterate_z / jnp.sqrt(norm_scale)
    moved = dot_stacked(root_inv, back_anom)
    pull = dot_split(root_inv, jnp.broadcast_to(residual, (ensemble, 128)))[:, :1]
    shift = back_mean + jnp.sum(pull * moved, axis=0, keepdims=True)
    analysed = shift + (ensemble - 1.0) ** 0.5 * moved

    for k in range(n_member):
        rows_k = analysed[k * members : (k + 1) * members]
        back_out[k] = jnp.concatenate(
            [rows_k[:, f * width : (f + 1) * width] for f in range(fields)], axis=0
        ).astype(BF16)
    for i in range(1, n_member):
        target = member_at(i)
        copy = pltpu.make_async_remote_copy(
            src_ref=back_out.at[target],
            dst_ref=back_in.at[me],
            send_sem=back_send,
            recv_sem=back_recv,
            device_id=(target, tile),
            device_id_type=MESH,
        )
        copy.start()
    back_in[me] = back_out[me]
    for copy in halo_copies:
        copy.wait_send()
    for s in range(3):
        for half in range(halves):
            packets = outbox.at[half, pl.ds(0, arriving(s))]
            pltpu.make_async_copy(packets, packets, fore_send.at[s, half]).wait()
    packets = back_in.at[pl.ds(0, n_member - 1)]
    pltpu.make_async_copy(packets, packets, back_recv).wait()
    out_ref[...] = back_in[...]
    packets = back_out.at[pl.ds(0, n_member - 1)]
    pltpu.make_async_copy(packets, packets, back_send).wait()


def local(state, first_weight, middle_weight, last_weight, observations, obs_variance, observation_rows, loc_class):
    members, fields, rows, width = state.shape
    channels = first_weight.shape[0]
    middle = middle_weight.shape[0]
    depth = middle + 2
    n_member = lax.axis_size("member")
    n_tile = lax.axis_size("tile")
    assert rows == n_member and n_tile >= 3
    kept = depth
    while fields * kept % 16:
        kept += 1
    assert kept <= rows and rows > 4
    block = fields * rows
    first_rows = rows + 2 * (depth - 1)
    obs = observations.shape[2]
    span = fields * width
    whole_lines = [(f, depth - kept + q) for f in range(fields) for q in range(kept)]
    own_lines = [(f, depth + r) for f in range(fields) for r in range(rows)]
    whole_lines += own_lines + [(f, depth + rows + q) for f in range(fields) for q in range(kept)]
    own_rows = range(depth, depth + rows - 2)
    edge_rows = [r for r in range(first_rows) if r not in own_rows]
    lanes = tuple(-(-3 * len(lines) // 128) * 128 for lines in (whole_lines, own_lines))
    spread = jnp.asarray(
        np.concatenate(
            [
                first_selector(fields, whole_lines, edge_rows, lanes[0]),
                first_selector(fields, own_lines, own_rows, lanes[1]),
            ],
            axis=1,
        ),
        BF16,
    )
    operands = (
        state.reshape(members, block, width),
        spread,
        jnp.transpose(first_weight, (2, 3, 1, 0)).reshape(9, fields, channels),
        jnp.transpose(middle_weight, (0, 3, 4, 1, 2)).reshape(9 * middle, channels, channels),
        jnp.transpose(last_weight, (2, 3, 0, 1)).reshape(9, fields, channels),
        observations[0],
        obs_variance[0],
        observation_rows[0],
        loc_class[0],
    )
    halves = 1
    chunks = []
    for n in range(middle):
        out_rows = rows + 2 * (depth - 2 - n) if n else rows - 4
        most = max(1, 256 // channels - 2)
        chunks.append(max(c for c in range(1, out_rows + 1) if out_rows % c == 0 and c <= most))
    sizes = (n_member, n_tile, members, fields, rows, width, channels, depth, kept, lanes, halves, chunks)
    vmem = pl.BlockSpec(memory_space=pltpu.VMEM)
    packet = (fields * members, width)
    out = pl.pallas_call(
        functools.partial(kernel, sizes),
        out_shape=pltpu.VMEM((rows, *packet), BF16),
        in_specs=[pl.BlockSpec(memory_space=pltpu.HBM)] * len(operands),
        out_specs=vmem,
        scratch_shapes=[
            *[pltpu.VMEM(v.shape, v.dtype) for v in operands],
            pltpu.VMEM((2 * depth * channels, 3 * len(whole_lines)), BF16),
            pltpu.VMEM(((rows - 2) * channels, 3 * len(own_lines)), BF16),
            pltpu.VMEM((3 * depth * channels, (depth + 2) * channels), BF16),
            *[
                pltpu.VMEM((3 * chunks[n] * channels, (chunks[n] + 2) * channels), BF16)
                for n in range(middle)
            ],
            pltpu.VMEM((3 * block, (rows + 2) * channels), BF16),
            pltpu.VMEM((members * block, width), F32),
            pltpu.VMEM((3, span, obs), BF16),
            pltpu.VMEM((2, members, fields * kept, width), BF16),
            pltpu.VMEM((2, members, fields * kept, width), BF16),
            pltpu.VMEM((halves, n_member, fields * members // halves, width), BF16),
            pltpu.VMEM((3, halves, n_member, fields * members // halves, width), BF16),
            pltpu.VMEM((n_member, *packet), BF16),
            pltpu.VMEM((n_member, *packet), BF16),
            pltpu.SemaphoreType.DMA((len(operands),)),
            pltpu.SemaphoreType.DMA((2,)),
            pltpu.SemaphoreType.DMA((2,)),
            pltpu.SemaphoreType.DMA((3, halves)),
            pltpu.SemaphoreType.DMA((3, halves)),
            pltpu.SemaphoreType.DMA,
            pltpu.SemaphoreType.DMA,
        ],
        compiler_params=pltpu.CompilerParams(
            collective_id=0, has_side_effects=True, vmem_limit_bytes=60 * 1024 * 1024
        ),
    )(*operands)
    return jnp.transpose(out.reshape(rows, fields, members, width), (2, 1, 0, 3))


def solution(mesh):
    return jax.shard_map(
        local,
        mesh=mesh,
        in_specs=(
            P("member", None, "tile", None),
            P(),
            P(),
            P(),
            P("tile", "member", None),
            P("tile", "member", None),
            P("tile", "member", None),
            P("tile", "member", None),
        ),
        out_specs=P("member", None, "tile", None),
        check_vma=False,
    )
```

```python
import functools

import jax
import jax.numpy as jnp
import numpy as np
from jax import lax
from jax.experimental import pallas as pl
from jax.experimental.pallas import tpu as pltpu
from jax.sharding import PartitionSpec as P

NS_ITERS = 4
MESH = pl.DeviceIdType.MESH
F32 = jnp.float32
BF16 = jnp.bfloat16


def silu(v):
    half = 0.5 * v
    return half + half * jnp.tanh(half)


def first_selector(fields, where, out_rows, lanes):
    spread = np.zeros((3, 3, fields, len(out_rows), lanes), np.float32)
    for dx in range(3):
        for k, (f, row) in enumerate(where):
            for n, r in enumerate(out_rows):
                if 0 <= row - r <= 2:
                    spread[row - r, dx, f, n, dx * len(where) + k] = 1
    return spread.reshape(9 * fields, len(out_rows) * lanes)


def middle_layer(taps, hidden, chunk, channels, width):
    count = hidden.shape[0] // channels - 2
    parts = [
        silu(gathered(dot(taps, hidden[r * channels : (r + chunk + 2) * channels]), width)).astype(BF16)
        for r in range(0, count, chunk)
    ]
    return jnp.concatenate(parts, axis=0)


def spread_middle(taps, base, chunk, channels):
    inner = (chunk + 2) * channels
    for r in range(chunk):
        moved = (pltpu.roll(base, r * channels, 1) if r else base).astype(BF16)
        for dx in range(3):
            at = (dx * chunk + r) * channels
            taps[at : at + channels, :] = moved[dx * channels : (dx + 1) * channels, :inner]


def dot(a, b):
    return jnp.dot(a, b, preferred_element_type=F32)


def split(v):
    high = v.astype(BF16)
    return high, (v - high.astype(F32)).astype(BF16)


def stacked_parts(b):
    high, low = split(b)
    return jnp.concatenate([high, high, low, low], axis=0)


def dot_split(a_twice, b):
    return dot_stacked(a_twice, stacked_parts(b))


def dot_stacked(a_twice, b_parts):
    high, low = split(a_twice)
    size = a_twice.shape[0]
    lane = lax.broadcasted_iota(jnp.int32, a_twice.shape, 1)
    mixed = jnp.where(lane < size, high.astype(F32), low.astype(F32)).astype(BF16)
    return dot(jnp.concatenate([mixed, mixed], axis=1), b_parts)


def shifted(v):
    width = v.shape[1]
    return jnp.concatenate([pltpu.roll(v, 1, 1), v, pltpu.roll(v, width - 1, 1)], axis=0)


def gathered(parts, width):
    third = parts.shape[0] // 3
    sums = []
    for at in range(0, parts.shape[1], width):
        part = parts[:, at : at + width]
        left, right = pltpu.roll(part[:third], 1, 1), pltpu.roll(part[2 * third :], width - 1, 1)
        sums.append(part[third : 2 * third] + left + right)
    return jnp.concatenate(sums, axis=1)


def tap_rows(load, padded):
    lines = []
    for dx in range(3):
        parts = [load(3 * dy + dx) for dy in range(3)]
        filler = jnp.zeros((parts[0].shape[0], padded - 3 * parts[0].shape[1]), F32)
        lines.append(jnp.concatenate([*parts, filler], axis=1))
    return jnp.concatenate(lines, axis=0)


def kernel(sizes, *refs):
    n_member, n_tile, members, fields, rows, width, channels, depth, kept, lanes, halves, chunks = sizes
    edge_lanes, own_lanes = lanes
    middle = depth - 2
    sources, out_ref, refs = refs[:9], refs[9], refs[10:]
    fetched, refs = refs[:9], refs[9:]
    (
        state_ref, spread_ref, first_ref, middle_ref, last_ref, observed_ref, variance_ref, rows_ref, class_ref,
    ) = fetched
    taps_first, taps_own, taps_edge, refs = refs[0], refs[1], refs[2], refs[3:]
    taps_middle, refs = refs[:middle], refs[middle:]
    (
        taps_last, mixed, onehot, halo_out, halo_in, outbox, inbox, back_out, back_in, fetch_sem,
        halo_send, halo_recv, fore_send, fore_recv, back_send, back_recv,
    ) = refs
    fetches = [
        pltpu.make_async_copy(source, target, fetch_sem.at[n])
        for n, (source, target) in enumerate(zip(sources, fetched))
    ]
    fetches[0].start()
    me = lax.axis_index("member")
    tile = lax.axis_index("tile")
    block = fields * rows
    ensemble = n_member * members
    span = fields * width

    def wrapped(index, count):
        index = jnp.where(index >= count, index - count, index)
        return jnp.where(index < 0, index + count, index)

    def tile_at(shift):
        return wrapped(tile + shift, n_tile) if shift else tile

    def member_at(shift):
        return wrapped(me + shift, n_member) if shift else me

    barrier = pltpu.get_barrier_semaphore()
    peers = [(i, d) for d in (1, -1, 0) for i in range(n_member) if (i, d) != (0, 0)]
    for i, d in peers:
        pl.semaphore_signal(barrier, inc=1, device_id=(member_at(i), tile_at(d)), device_id_type=MESH)

    for fetch in fetches[1:]:
        fetch.start()
    fetches[0].wait()
    for m in range(members):
        whole = state_ref[m].astype(F32)
        each = [whole[f * rows : (f + 1) * rows] for f in range(fields)]
        halo_out[0, m] = jnp.concatenate([v[rows - kept :] for v in each], axis=0).astype(BF16)
        halo_out[1, m] = jnp.concatenate([v[:kept] for v in each], axis=0).astype(BF16)
    with jax.named_scope("taps"):
        for fetch in fetches[1:]:
            fetch.wait()
        first_taps = jnp.concatenate([first_ref[n].astype(F32) for n in range(9)], axis=0).astype(BF16)
        wide = lax.dot_general(
            first_taps, spread_ref[...], (((0,), (0,)), ((), ())), preferred_element_type=F32
        ).astype(BF16)
        count = taps_first.shape[1]
        for r in range(2 * depth):
            taps_first[r * channels : (r + 1) * channels, :] = wide[:, r * edge_lanes : r * edge_lanes + count]
        begin = 2 * depth * edge_lanes
        count = taps_own.shape[1]
        for r in range(rows - 2):
            taps_own[r * channels : (r + 1) * channels, :] = wide[:, begin + r * own_lanes : begin + r * own_lanes + count]
        for number in range(middle):
            chunk = max(chunks[number], depth)
            base = tap_rows(lambda n: middle_ref[9 * number + n].astype(F32), -(-(chunk + 2) * channels // 128) * 128)
            spread_middle(taps_middle[number], base, chunks[number], channels)
            if number == 0:
                spread_middle(taps_edge, base, depth, channels)
        inner = (rows + 2) * channels
        padded = -(-inner // 128) * 128
        base = tap_rows(lambda n: last_ref[n].astype(F32), padded)
        base = jnp.broadcast_to(base[:, None, :], (base.shape[0], rows, padded)).reshape(-1, padded)
        row_of = lax.rem(lax.broadcasted_iota(jnp.int32, base.shape, 0), rows)
        total = jnp.where(row_of == 0, base, 0.0)
        for r in range(1, rows):
            total = total + jnp.where(row_of == r, pltpu.roll(base, r * channels, 1), 0.0)
        taps_last[...] = total.astype(BF16)[:, :inner]

    pl.semaphore_wait(barrier, len(peers))
    halo_copies = []
    for side, d in ((0, 1), (1, -1)):
        copy = pltpu.make_async_remote_copy(
            src_ref=halo_out.at[side],
            dst_ref=halo_in.at[side],
            send_sem=halo_send.at[side],
            recv_sem=halo_recv.at[side],
            device_id=(me, tile_at(d)),
            device_id_type=MESH,
        )
        copy.start()
        halo_copies.append(copy)

    share = members // halves
    group = 2 if share % 2 == 0 else 1
    groups = [range(start, start + group) for start in range(0, members, group)]

    own_first = []
    for ids in groups:
        stacked = [shifted(state_ref[m].astype(F32)) for m in ids]
        own_first.append(silu(dot(taps_own[...], jnp.concatenate(stacked, axis=1).astype(BF16))).astype(BF16))
    own_second = [middle_layer(taps_middle[0][...], v, chunks[0], channels, width) for v in own_first]

    for copy in halo_copies:
        copy.wait_recv()

    for half in range(halves):
        edge_first = []
        for ids in groups:
            stacked = [
                shifted(jnp.concatenate([halo_in[0, m], state_ref[m], halo_in[1, m]], axis=0).astype(F32))
                for m in ids
            ]
            edge_first.append(silu(dot(taps_first[...], jnp.concatenate(stacked, axis=1).astype(BF16))).astype(BF16))
        hidden = []
        cut = depth * channels
        for edge, own, second in zip(edge_first, own_first, own_second):
            above = jnp.concatenate([edge[:cut], own[: 2 * channels]], axis=0)
            below = jnp.concatenate([own[(rows - 4) * channels :], edge[cut:]], axis=0)
            above = middle_layer(taps_edge[...], above, depth, channels, width)
            below = middle_layer(taps_edge[...], below, depth, channels, width)
            hidden.append(jnp.concatenate([above, second, below], axis=0))
        for number in range(1, middle):
            hidden = [middle_layer(taps_middle[number][...], v, chunks[number], channels, width) for v in hidden]
        for ids, before in zip(groups, hidden):
            change = gathered(dot(taps_last[...], before), width)
            for g, m in enumerate(ids):
                mixed[m * block : (m + 1) * block, :] = (
                    state_ref[m].astype(F32) + change[:, g * width : (g + 1) * width]
                )

        for r in range(rows):
            outbox[half, r] = jnp.concatenate(
                [mixed[pl.ds(half * share * block + f * rows + r, share, stride=block), :] for f in range(fields)],
                axis=0,
            ).astype(BF16)

        for s in (0, 2, 1):
            for i in range(n_member):
                if s == 1 and i == 0:
                    continue
                target = member_at(i)
                copy = pltpu.make_async_remote_copy(
                    src_ref=outbox.at[half, target],
                    dst_ref=inbox.at[s, half, me],
                    send_sem=fore_send.at[s, half],
                    recv_sem=fore_recv.at[s, half],
                    device_id=(target, tile_at(1 - s)),
                    device_id_type=MESH,
                )
                copy.start()
        inbox[1, half, me] = outbox[half, me]

    read = rows_ref[...]
    spot = lax.broadcasted_iota(jnp.int32, (span, read.shape[1]), 0)
    for s in range(3):
        onehot[s] = jnp.where(spot == read - s * span, 1.0, 0.0).astype(BF16)
    obs_weight = jnp.exp(-0.25 * class_ref[...].astype(F32)) / variance_ref[...]
    obs_root = jnp.sqrt(obs_weight)
    eye_row = lax.broadcasted_iota(jnp.int32, (ensemble, 2 * ensemble), 0)
    eye_col = lax.broadcasted_iota(jnp.int32, (ensemble, 2 * ensemble), 1)
    identity = jnp.where((eye_row == eye_col) | (eye_row + ensemble == eye_col), 1.0, 0.0).astype(F32)

    def neighbour(s):
        blocks = [inbox[s, half, k].astype(F32) for k in range(n_member) for half in range(halves)]
        columns = [
            jnp.concatenate([b[f * share : (f + 1) * share] for b in blocks], axis=0) for f in range(fields)
        ]
        return jnp.concatenate(columns, axis=1)

    def arriving(s):
        return n_member - 1 if s == 1 else n_member

    obs_ens = None
    for s in (1, 0, 2):
        for half in range(halves):
            packets = inbox.at[s, half, pl.ds(0, arriving(s))]
            pltpu.make_async_copy(packets, packets, fore_recv.at[s, half]).wait()
        values = neighbour(s)
        if s == 1:
            back_mean = jnp.sum(values, axis=0, keepdims=True) / ensemble
            back_anom = stacked_parts(values - back_mean)
        part = dot(values.astype(BF16), onehot[s])
        obs_ens = part if obs_ens is None else obs_ens + part

    obs_mean = jnp.sum(obs_ens, axis=0, keepdims=True) / ensemble
    obs_anom = obs_ens - obs_mean
    parts = jnp.concatenate(split(obs_root * obs_anom), axis=0)
    quadrants = lax.dot_general(parts, parts, (((1,), (1,)), ((), ())), preferred_element_type=F32)
    beside = quadrants[:ensemble] + quadrants[ensemble:]
    gram = (ensemble - 1.0) * identity + (beside + pltpu.roll(beside, ensemble, 1))
    residual = jnp.sum(obs_anom * (obs_weight * (observed_ref[...] - obs_mean)), axis=1, keepdims=True)
    norm_scale = jnp.sqrt(0.5 * jnp.sum(gram * gram, keepdims=True))
    iterate_y = gram / norm_scale
    iterate_z = 1.5 * identity - 0.5 * iterate_y
    iterate_y = dot_split(iterate_y, iterate_z)
    for sweep in range(1, NS_ITERS):
        factor = 1.5 * identity - 0.5 * dot_split(iterate_z, iterate_y)
        if sweep + 1 < NS_ITERS:
            iterate_y = dot_split(iterate_y, factor)
        iterate_z = dot_split(factor, iterate_z)
    root_inv = iterate_z / jnp.sqrt(norm_scale)
    moved = dot_stacked(root_inv, back_anom)
    pull = dot_split(root_inv, jnp.broadcast_to(residual, (ensemble, 128)))[:, :1]
    shift = back_mean + jnp.sum(pull * moved, axis=0, keepdims=True)
    analysed = shift + (ensemble - 1.0) ** 0.5 * moved

    for k in range(n_member):
        rows_k = analysed[k * members : (k + 1) * members]
        back_out[k] = jnp.concatenate(
            [rows_k[:, f * width : (f + 1) * width] for f in range(fields)], axis=0
        ).astype(BF16)
    for i in range(1, n_member):
        target = member_at(i)
        copy = pltpu.make_async_remote_copy(
            src_ref=back_out.at[target],
            dst_ref=back_in.at[me],
            send_sem=back_send,
            recv_sem=back_recv,
            device_id=(target, tile),
            device_id_type=MESH,
        )
        copy.start()
    back_in[me] = back_out[me]
    for copy in halo_copies:
        copy.wait_send()
    for s in range(3):
        for half in range(halves):
            packets = outbox.at[half, pl.ds(0, arriving(s))]
            pltpu.make_async_copy(packets, packets, fore_send.at[s, half]).wait()
    packets = back_in.at[pl.ds(0, n_member - 1)]
    pltpu.make_async_copy(packets, packets, back_recv).wait()
    out_ref[...] = back_in[...]
    packets = back_out.at[pl.ds(0, n_member - 1)]
    pltpu.make_async_copy(packets, packets, back_send).wait()


def local(state, first_weight, middle_weight, last_weight, observations, obs_variance, observation_rows, loc_class):
    members, fields, rows, width = state.shape
    channels = first_weight.shape[0]
    middle = middle_weight.shape[0]
    depth = middle + 2
    n_member = lax.axis_size("member")
    n_tile = lax.axis_size("tile")
    assert rows == n_member and n_tile >= 3
    kept = depth
    while fields * kept % 16:
        kept += 1
    assert kept <= rows and rows > 4
    block = fields * rows
    first_rows = rows + 2 * (depth - 1)
    obs = observations.shape[2]
    span = fields * width
    whole_lines = [(f, depth - kept + q) for f in range(fields) for q in range(kept)]
    own_lines = [(f, depth + r) for f in range(fields) for r in range(rows)]
    whole_lines += own_lines + [(f, depth + rows + q) for f in range(fields) for q in range(kept)]
    own_rows = range(depth, depth + rows - 2)
    edge_rows = [r for r in range(first_rows) if r not in own_rows]
    lanes = tuple(-(-3 * len(lines) // 128) * 128 for lines in (whole_lines, own_lines))
    spread = jnp.asarray(
        np.concatenate(
            [
                first_selector(fields, whole_lines, edge_rows, lanes[0]),
                first_selector(fields, own_lines, own_rows, lanes[1]),
            ],
            axis=1,
        ),
        BF16,
    )
    operands = (
        state.reshape(members, block, width),
        spread,
        jnp.transpose(first_weight, (2, 3, 1, 0)).reshape(9, fields, channels),
        jnp.transpose(middle_weight, (0, 3, 4, 1, 2)).reshape(9 * middle, channels, channels),
        jnp.transpose(last_weight, (2, 3, 0, 1)).reshape(9, fields, channels),
        observations[0],
        obs_variance[0],
        observation_rows[0],
        loc_class[0],
    )
    halves = 1
    chunks = []
    for n in range(middle):
        out_rows = rows + 2 * (depth - 2 - n) if n else rows - 4
        most = max(1, 256 // channels - 2)
        chunks.append(max(c for c in range(1, out_rows + 1) if out_rows % c == 0 and c <= most))
    sizes = (n_member, n_tile, members, fields, rows, width, channels, depth, kept, lanes, halves, chunks)
    vmem = pl.BlockSpec(memory_space=pltpu.VMEM)
    packet = (fields * members, width)
    out = pl.pallas_call(
        functools.partial(kernel, sizes),
        out_shape=pltpu.VMEM((rows, *packet), BF16),
        in_specs=[pl.BlockSpec(memory_space=pltpu.HBM)] * len(operands),
        out_specs=vmem,
        scratch_shapes=[
            *[pltpu.VMEM(v.shape, v.dtype) for v in operands],
            pltpu.VMEM((2 * depth * channels, 3 * len(whole_lines)), BF16),
            pltpu.VMEM(((rows - 2) * channels, 3 * len(own_lines)), BF16),
            pltpu.VMEM((3 * depth * channels, (depth + 2) * channels), BF16),
            *[
                pltpu.VMEM((3 * chunks[n] * channels, (chunks[n] + 2) * channels), BF16)
                for n in range(middle)
            ],
            pltpu.VMEM((3 * block, (rows + 2) * channels), BF16),
            pltpu.VMEM((members * block, width), F32),
            pltpu.VMEM((3, span, obs), BF16),
            pltpu.VMEM((2, members, fields * kept, width), BF16),
            pltpu.VMEM((2, members, fields * kept, width), BF16),
            pltpu.VMEM((halves, n_member, fields * members // halves, width), BF16),
            pltpu.VMEM((3, halves, n_member, fields * members // halves, width), BF16),
            pltpu.VMEM((n_member, *packet), BF16),
            pltpu.VMEM((n_member, *packet), BF16),
            pltpu.SemaphoreType.DMA((len(operands),)),
            pltpu.SemaphoreType.DMA((2,)),
            pltpu.SemaphoreType.DMA((2,)),
            pltpu.SemaphoreType.DMA((3, halves)),
            pltpu.SemaphoreType.DMA((3, halves)),
            pltpu.SemaphoreType.DMA,
            pltpu.SemaphoreType.DMA,
        ],
        compiler_params=pltpu.CompilerParams(
            collective_id=0, has_side_effects=True, vmem_limit_bytes=60 * 1024 * 1024
        ),
    )(*operands)
    return jnp.transpose(out.reshape(rows, fields, members, width), (2, 1, 0, 3))


def solution(mesh):
    return jax.shard_map(
        local,
        mesh=mesh,
        in_specs=(
            P("member", None, "tile", None),
            P(),
            P(),
            P(),
            P("tile", "member", None),
            P("tile", "member", None),
            P("tile", "member", None),
            P("tile", "member", None),
        ),
        out_specs=P("member", None, "tile", None),
        check_vma=False,
    )
```
